32 devices in a mesh: groups: 2 (over y), tensor: 4 (over z), store: 4 (over x, core).
Axes of the slice: x: 2, y: 2, z: 4, core: 2. Of those that a mesh axis runs over, the one named last changes fastest.
Arguments:
- attention_input: bfloat16 [128, 16, 8192], P(('groups', 'store'), None, 'tensor'), parts along dimension 0, may hold values from -6 to 6
- base_projection_weight: bfloat16 [8192, 8192], P('tensor', 'store'), may hold values from -0.0625 to 0.0625
- stored_down_maps: bfloat16 [64, 8192, 64], P('store', 'tensor'), may hold values from -0.0625 to 0.0625
- stored_up_maps: bfloat16 [64, 64, 8192], P('store', None, 'tensor'), may hold values from -0.75 to 0.75
- request_adapter_index: int32 [128], P('groups'), parts along dimension 0, may hold values from 0 to 63, as said below
- adapter_store_slot: int32 [128], P('groups'), parts along dimension 0, may hold values from 0 to 63, as said below
- lengths: int32 [128], P(('groups', 'store')), parts along dimension 0, may hold values from 1 to 16, 768 in all
Outputs:
- projected: bfloat16 [128, 16, 8192], P(('groups', 'store'), None, 'tensor'), parts along dimension 0
The draws below stay inside these ranges and needn't reach their ends.
There are 2 independent parts, one for each index of `groups`. The reference program is written for one: setup_inputs(seed, part) draws one part's arguments, and reference() takes and returns one part's arrays. A program takes and returns all parts, laid end to end along the dimension named above; an argument that names none is the same for every part. Nothing has to cross between parts.
Inputs may be any that keep to these rules, and one draw needn't show every extreme that they name: adapter_store_slot is a permutation of the 64 slots. `request_adapter_index`: among the 16 requests of one store index, at most 8 have adapters of one owner, and some owner has exactly 8 of them.
All inputs are finite; a program needn't handle non-finite values. No bound on the sum of `lengths` on one device may be relied on, other than what follows from the above.
Results may differ from the reference program's by a relative error of at most 0.015.
Values may be sent and summed in bfloat16 or wider, within the bound.
No kernel may reach another device: no remote copies, remote signals or barrier semaphores. Data moves between devices by JAX's collectives and lax.ppermute only.
A program may use at most 192 MiB of HBM per device.

```python
import math
import jax
import jax.numpy as jnp
import numpy as np
from jax import lax

MODEL_WIDTH = 8192
INPUT_FEATURES = 8192
ADAPTER_RANK = 64
SEQ = 16
REQ_DEV = 16
AD_DEV = 16
CAP = 8
REQUESTS = 64
ADAPTER_COUNT = 64
N_TENSOR = 4
N_STORE = 4


def shared_slots(key):
    return jax.random.permutation(key, ADAPTER_COUNT).astype(jnp.int32)


def draw_adapter_store_slot(key, part):
    return shared_slots(key)


def draw_request_adapter_index(key, part):
    slot_perm = shared_slots(key)
    key = jax.random.fold_in(key, 7)
    key_pop, key_noise, key_local, key_order = jax.random.split(key, 4)
    owner_range = jnp.arange(N_STORE, dtype=jnp.int32)
    popular = jax.random.randint(key_pop, (N_STORE,), 0, 2 * N_STORE)
    noise = jax.random.randint(key_noise, (N_STORE, N_STORE), 0, N_STORE)
    scores = (popular[None, :] + noise) * N_STORE + owner_range[None, :]
    ordered = jnp.argsort(scores, axis=1, stable=True).astype(jnp.int32)
    pool = jnp.repeat(ordered, CAP, axis=1)
    owners = pool[:, :REQ_DEV]
    owners = jax.random.permutation(key_order, owners, axis=1, independent=True)
    local_slot = jax.random.randint(key_local, (N_STORE, REQ_DEV), 0, AD_DEV)
    target_slot = owners * AD_DEV + local_slot
    inverse = jnp.argsort(slot_perm, stable=True).astype(jnp.int32)
    return inverse[target_slot.reshape(REQUESTS)].astype(jnp.int32)


def steps_of(rng, dims, cuts, low, high):
    loudness = 1.0
    for position, blocks in cuts:
        steps = jax.random.uniform(jax.random.fold_in(jax.random.fold_in(rng, 6), position), (blocks,), jnp.float32, low / len(cuts), high / len(cuts))
        loudness = loudness * jnp.repeat(jnp.exp(steps), dims[position] // blocks).reshape((-1,) + (1,) * (len(dims) - 1 - position))
    return loudness


def split_up(count, total, reach, lean):
    portions = [(1 << 20) // math.isqrt(rank ** lean) + 1 for rank in range(2, count + 1)]
    rest, given = total - reach - (count - 1), [1] * (count - 1)
    while rest > 0:
        candidates = [i for i in range(count - 1) if given[i] < reach]
        whole, remaining = sum([portions[i] for i in candidates]), rest
        for i in candidates:
            more = min(reach - given[i], max(1, remaining * portions[i] // whole), rest)
            given[i] = given[i] + more
            rest = rest - more
    return np.array([reach] + given)


def uneven(key, amount, total, bound, skew):
    if amount == 2:
        one = jax.random.randint(key, (), max(1, total - bound), min(bound, total - 1) + 1)
        return jnp.stack([one, total - one])
    sizes = jnp.asarray(split_up(amount, total, bound, skew), jnp.int32)
    pairs = (amount - 1) // 2
    giver, receiver = sizes[1:1 + 2 * pairs:2], sizes[2:2 + 2 * pairs:2]
    margin = jnp.minimum(giver - 1, bound - receiver)
    moved = jax.random.randint(jax.random.fold_in(key, 1), (pairs,), 0, 1 << 20) % (margin + 1)
    sizes = sizes.at[1:1 + 2 * pairs:2].set(giver - moved).at[2:2 + 2 * pairs:2].set(receiver + moved)
    return sizes[jax.random.permutation(jax.random.fold_in(key, 2), amount)]


def normal_values(stream_key, shape, deviation, bound, shards=(), held_as=jnp.bfloat16):
    gain = steps_of(stream_key, shape, shards, -0.22, 0.18) if shards else 1.0
    array = jax.random.normal(stream_key, shape, jnp.float32) * deviation * gain
    return jnp.minimum(jnp.maximum(array, -bound), bound).astype(held_as)


def setup_inputs(seed: int = 0, part: int = 0) -> dict:
    seeds = jax.random.split(jax.random.key(seed), 8)
    own_keys = jax.random.split(jax.random.fold_in(seeds[7], part), 8)
    attention_input = normal_values(own_keys[0], (REQUESTS, SEQ, INPUT_FEATURES), 1.0, 6.0, ((0, 4), (2, 4)))
    base_projection_weight = normal_values(seeds[1], (INPUT_FEATURES, MODEL_WIDTH), INPUT_FEATURES ** -0.5, 0.0625, ((0, 4), (1, 4)))
    stored_down_maps = normal_values(seeds[2], (ADAPTER_COUNT, INPUT_FEATURES, ADAPTER_RANK), INPUT_FEATURES ** -0.5, 0.0625, ((0, 4), (1, 4)))
    stored_up_maps = normal_values(seeds[3], (ADAPTER_COUNT, ADAPTER_RANK, MODEL_WIDTH), ADAPTER_RANK ** -0.5, 0.75, ((0, 4), (2, 4)))
    request_adapter_index = draw_request_adapter_index(jax.random.fold_in(jax.random.fold_in(seeds[7], part), 71), part)
    adapter_store_slot = draw_adapter_store_slot(jax.random.fold_in(jax.random.fold_in(seeds[7], part), 71), part)
    lengths = uneven(own_keys[6], REQUESTS, REQUESTS * SEQ * 3 // 4, SEQ, 1).astype(jnp.int32)
    return dict(attention_input=attention_input, base_projection_weight=base_projection_weight, stored_down_maps=stored_down_maps, stored_up_maps=stored_up_maps, request_adapter_index=request_adapter_index, adapter_store_slot=adapter_store_slot, lengths=lengths)


def reference(attention_input, base_projection_weight, stored_down_maps, stored_up_maps, request_adapter_index, adapter_store_slot, lengths):
    flat_rows = attention_input.reshape(REQUESTS * SEQ, INPUT_FEATURES)
    block_width = INPUT_FEATURES // N_TENSOR
    base_sum = jnp.zeros((REQUESTS * SEQ, MODEL_WIDTH), jnp.float32)
    for tile_index in range(N_TENSOR):
        lower = tile_index * block_width
        partial_value = jnp.dot(flat_rows[:, lower:lower + block_width], base_projection_weight[lower:lower + block_width], preferred_element_type=jnp.float32)
        rounded = lax.optimization_barrier(partial_value.astype(jnp.bfloat16))
        base_sum = base_sum + rounded.astype(jnp.float32)
    store_slot_rows = adapter_store_slot[request_adapter_index].astype(jnp.int32)
    down_map_rows = stored_down_maps[store_slot_rows].astype(jnp.float32)
    up_map_rows = stored_up_maps[store_slot_rows].astype(jnp.float32)
    low_rank = jnp.einsum('qtk,qkr->qtr', attention_input.astype(jnp.float32), down_map_rows).astype(jnp.bfloat16)
    delta_rows = jnp.einsum('qtr,qrd->qtd', low_rank.astype(jnp.float32), up_map_rows).astype(jnp.bfloat16)
    positions = jnp.arange(SEQ, dtype=jnp.int32)
    valid_mask = (positions[None, :] < lengths[:, None]).astype(jnp.float32)
    total = base_sum.reshape(REQUESTS, SEQ, MODEL_WIDTH) + 2.0 * delta_rows.astype(jnp.float32)
    return (total * valid_mask[:, :, None]).astype(jnp.bfloat16)
```

```python
import functools
import jax
import jax.numpy as jnp
from jax import lax
from jax.experimental import pallas as pl
from jax.experimental.pallas import tpu as pltpu
from jax.sharding import PartitionSpec as P

VMEM_LIMIT = 48 * 1024 * 1024
STREAMS = 2
CHUNK = 64
BF16 = jnp.bfloat16
F32 = jnp.float32


def general(
    attention_input,
    base_projection_weight,
    stored_down_maps,
    stored_up_maps,
    request_adapter_index,
    adapter_store_slot,
    lengths,
):
    requests, seq_len, width_in = attention_input.shape
    owner_grouping = stored_down_maps.shape[0]
    stores = lax.axis_size("store")
    my_index = lax.axis_index("store")
    capacity = (2 * requests + stores - 1) // stores
    partial_value = jnp.einsum(
        "qtk,kd->qtd",
        attention_input,
        lax.all_gather(base_projection_weight, "store", axis=1, tiled=True),
        preferred_element_type=jnp.float32,
    )
    base_out = lax.psum_scatter(
        partial_value.astype(jnp.bfloat16), "tensor", scatter_dimension=2, tiled=True
    ).astype(jnp.float32)
    slot_all = adapter_store_slot[request_adapter_index]
    owner_all = (slot_all // owner_grouping).reshape(stores, requests)
    local_all = (slot_all % owner_grouping).reshape(stores, requests)
    positions = jnp.arange(requests, dtype=jnp.int32)
    earlier = positions[None, :] < positions[:, None]
    same_owner = owner_all[:, :, None] == owner_all[:, None, :]
    rank_all = jnp.sum(same_owner & earlier[None], axis=2)
    owner_mine = lax.dynamic_index_in_dim(owner_all, my_index, 0, keepdims=False)
    rank_mine = lax.dynamic_index_in_dim(rank_all, my_index, 0, keepdims=False)
    owner_range = jnp.arange(stores, dtype=jnp.int32)
    slot_range = jnp.arange(capacity, dtype=jnp.int32)
    local_range = jnp.arange(owner_grouping, dtype=jnp.int32)
    pick_table = (
        (owner_mine[:, None, None] == owner_range[None, :, None])
        & (rank_mine[:, None, None] == slot_range[None, None, :])
    ).astype(jnp.bfloat16)
    selection_matrix = jnp.sum(
        (
            (owner_all == my_index)[:, :, None, None]
            & (rank_all[:, :, None, None] == slot_range[None, None, :, None])
            & (local_all[:, :, None, None] == local_range[None, None, None, :])
        ).astype(jnp.float32),
        axis=1,
    ).astype(jnp.bfloat16)
    outgoing = jnp.einsum(
        "qoc,qtk->octk", pick_table, attention_input, preferred_element_type=jnp.float32
    ).astype(jnp.bfloat16)
    arrived = lax.all_to_all(outgoing, "store", split_axis=0, concat_axis=0, tiled=True)
    down_sel = jnp.einsum(
        "pmb,bwf->pmwf", selection_matrix, stored_down_maps, preferred_element_type=jnp.float32
    ).astype(jnp.bfloat16)
    up_sel = jnp.einsum(
        "ehw,wkx->ehkx", selection_matrix, stored_up_maps, preferred_element_type=jnp.float32
    ).astype(jnp.bfloat16)
    low_part = jnp.einsum("octk,ockr->octr", arrived, down_sel, preferred_element_type=jnp.float32)
    low_full = lax.psum(low_part.astype(jnp.bfloat16), "tensor")
    delta_rows = jnp.einsum(
        "octr,ocrd->octd", low_full, up_sel, preferred_element_type=jnp.float32
    ).astype(jnp.bfloat16)
    returned = lax.all_to_all(delta_rows, "store", split_axis=0, concat_axis=0, tiled=True)
    my_delta = jnp.einsum("qoc,octd->qtd", pick_table, returned, preferred_element_type=jnp.float32)
    token_slots = jnp.arange(seq_len, dtype=jnp.int32)
    valid_mask = (token_slots[None, :] < lengths[:, None]).astype(jnp.float32)
    total = base_out + 2.0 * my_delta
    return (total * valid_mask[:, :, None]).astype(jnp.bfloat16)


def project_kernel(first, blocks, pos_ref, *refs):
    x_refs, w_ref, out_ref, packed = refs[:blocks], refs[blocks], refs[blocks + 1], refs[blocks + 2]
    rows = packed.shape[0]

    @pl.when(pl.program_id(0) == 0)
    def _():
        width = x_refs[0].shape[0]
        wanted = lax.broadcasted_iota(jnp.int32, (rows, width), 0) + first
        acc = None
        for b in range(blocks):
            pick = (pos_ref[:, b * width : (b + 1) * width] == wanted).astype(F32).astype(BF16)
            part = jnp.dot(pick, x_refs[b][...], preferred_element_type=F32)
            acc = part if acc is None else acc + part
        packed[...] = acc.astype(BF16)

    out_ref[...] = jnp.dot(packed[...], w_ref[...], preferred_element_type=F32).astype(BF16)


def project(pos, xs, w, first, rows, tile=512):
    depth, cols = w.shape
    blocks = len(xs)
    block_rows = xs[0].shape[0]
    return pl.pallas_call(
        functools.partial(project_kernel, first, blocks),
        grid=(cols // tile,),
        in_specs=[pl.BlockSpec(pos.shape, lambda j: (0, 0))]
        + [pl.BlockSpec((block_rows, depth), lambda j: (0, 0))] * blocks
        + [pl.BlockSpec((depth, tile), lambda j: (0, j))],
        out_specs=pl.BlockSpec((rows, tile), lambda j: (0, j)),
        out_shape=jax.ShapeDtypeStruct((rows, cols), BF16),
        scratch_shapes=[pltpu.VMEM((rows, depth), BF16)],
        compiler_params=pltpu.CompilerParams(vmem_limit_bytes=VMEM_LIMIT),
        cost_estimate=pl.CostEstimate(
            flops=2 * rows * depth * (cols + blocks * block_rows),
            bytes_accessed=2 * (depth * cols + rows * cols + blocks * block_rows * depth),
            transcendentals=0,
        ),
    )(pos, *xs, w)


def finish_kernel(pieces, deltas, base_pos_ref, delta_pos_ref, *refs):
    piece_refs, delta_refs, out_ref = refs[:pieces], refs[pieces : pieces + deltas], refs[-1]
    rows = base_pos_ref.shape[0]

    def add(acc, pos_ref, group, start, value):
        stack = jnp.concatenate([g[...] for g in group], axis=0) if len(group) > 1 else group[0][...]
        columns = lax.broadcasted_iota(jnp.int32, (rows, stack.shape[0]), 1) + start
        pick = jnp.where(pos_ref[...] == columns, F32(value), F32(0)).astype(BF16)
        part = jnp.dot(pick, stack, preferred_element_type=F32)
        return part if acc is None else acc + part

    acc = None
    for refs_, pos_ref, value in (
        (piece_refs, base_pos_ref, 1.0),
        (delta_refs, delta_pos_ref, 2.0),
    ):
        size = refs_[0].shape[0]
        step = max(1, 256 // size)
        for i in range(0, len(refs_), step):
            acc = add(acc, pos_ref, refs_[i : i + step], i * size, value)
    out_ref[...] = acc.astype(BF16)


def finish(base_pos, delta_pos, pieces, deltas, tile=512):
    rows = base_pos.shape[0]
    cols = pieces[0].shape[1]
    depth = sum(p.shape[0] for p in pieces) + sum(d.shape[0] for d in deltas)
    return pl.pallas_call(
        functools.partial(finish_kernel, len(pieces), len(deltas)),
        grid=(cols // tile,),
        in_specs=[pl.BlockSpec((rows, 1), lambda j: (0, 0))] * 2
        + [pl.BlockSpec((a.shape[0], tile), lambda j: (0, j)) for a in list(pieces) + list(deltas)],
        out_specs=pl.BlockSpec((rows, tile), lambda j: (0, j)),
        out_shape=jax.ShapeDtypeStruct((rows, cols), BF16),
        compiler_params=pltpu.CompilerParams(vmem_limit_bytes=VMEM_LIMIT),
        cost_estimate=pl.CostEstimate(
            flops=2 * rows * depth * cols, bytes_accessed=2 * (depth + rows) * cols, transcendentals=0
        ),
    )(base_pos, delta_pos, *pieces, *deltas)


def on_store(value, flip):
    return lax.ppermute(value, "store", [(i, i ^ flip) for i in range(4)])


def forward(s):
    return 1 if s >= 2 else -1


def plane(s, u):
    return u if s >= 2 else 3 - u


def last_step(s):
    return 3 if s in (0, 3) else 2


def on_mesh(value, pairs):
    return lax.ppermute(value, ("tensor", "store"), [(a * 4 + b, c * 4 + d) for (a, b), (c, d) in pairs])


def placed(lens, tokens):
    n = lens.shape[0]
    before = jnp.arange(n)[None, :] < jnp.arange(n)[:, None]
    return jnp.sum(jnp.where(before, lens[None, :], 0), axis=1), jnp.sum(lens)


def square(x, w, down, up, request_adapter_index, adapter_store_slot, lengths):
    requests, tokens, depth = x.shape
    rows = requests * tokens
    live = 3 * rows
    held, _, rank = down.shape
    capacity = requests // 2
    span = STREAMS * CHUNK
    steps = live // span
    early = rows // span * span

    s = lax.axis_index("store")
    t = lax.axis_index("tensor")
    chip = s // 2
    u = jnp.where(chip == 1, t, 3 - t)

    x_me = x.reshape(rows, depth)
    len_me = lengths
    len_sib = on_store(len_me, 1)
    x_sib = on_store(x_me, 1)
    x_far = on_store(x_me, 2)
    len_far = on_store(len_me, 2)
    len_fsib = on_store(len_me, 3)
    x_fsib = on_store(x_far, 1)
    xs = [x_me, x_sib, x_far, x_fsib]

    token = jnp.arange(tokens, dtype=jnp.int32)
    first_core = (s % 2) == 0
    starts = [placed(l, tokens) for l in (len_me, len_sib, len_far, len_fsib)]
    own = starts[0][1] + starts[1][1]
    offs = [
        jnp.where(first_core, 0, starts[1][1]),
        jnp.where(first_core, starts[0][1], 0),
        own + jnp.where(first_core, 0, starts[3][1]),
        own + jnp.where(first_core, starts[2][1], 0),
    ]

    def where_rows(block, length, offset):
        spot = block[:, None] + offset + token[None, :]
        return jnp.where(token[None, :] < length[:, None], spot, -(1 << 20))

    lens = [len_me, len_sib, len_far, len_fsib]
    pos = [where_rows(starts[i][0], lens[i], offs[i] + u * span).reshape(1, rows) for i in range(4)]
    pos_own = jnp.concatenate(pos[:2], axis=1)
    pos_all = jnp.concatenate(pos, axis=1)

    total_rows = live + 3 * span
    parts = [(0, project(pos_own, xs[:2], w, 0, early))]
    at = early
    while at < total_rows:
        size = min(early, total_rows - at)
        parts.append((at, project(pos_all, xs, w, at, size)))
        at += size

    def shifted(start, size):
        for base, value in parts:
            if base <= start and start + size <= base + value.shape[0]:
                return value[start - base : start - base + size]
        raise ValueError

    back_pairs = [((plane(b, 3), b), (plane(b, 2), b)) for b in (1, 2)]
    final = []
    carry = [None] * STREAMS
    for k in range(steps + 3):
        pairs = [
            ((plane(b, v), b), (plane(b, v + 1), b))
            for b in range(4)
            for v in range(last_step(b))
            if 0 <= k - v < steps
        ]
        for j in range(STREAMS):
            value = None
            if k < steps + 3:
                value = shifted(k * span + j * CHUNK, CHUNK)
            if carry[j] is not None or k >= 2:
                total = value.astype(F32)
                if carry[j] is not None:
                    total = total + carry[j].astype(F32)
                if 2 <= k < steps + 2:
                    back = on_mesh(shifted((k + 1) * span + j * CHUNK, CHUNK), back_pairs)
                    total = total + back.astype(F32)
                value = total.astype(BF16)
            if k >= 2:
                final.append((k, j, value))
            carry[j] = on_mesh(value, pairs) if pairs else None

    is_root = s == t
    across = [((v, v), (v, v ^ 2)) for v in range(4)]
    beside = [((v, v), (v, v ^ 1)) for v in range(4)] + [((v, v ^ 2), (v, v ^ 3)) for v in range(4)]
    pieces = []
    for k, j, value in final:
        if k >= 2 + rows // span:
            value = jnp.where(is_root, value, on_mesh(value, across))
        elif k == 2 + rows // span - 1 or k == 2:
            value = value
        got = on_mesh(value, beside)
        keep = is_root | (s == (t ^ 2))
        pieces.append(jnp.where(keep, value, got))

    slot_all = adapter_store_slot[request_adapter_index]
    owner_all = (slot_all // held).reshape(4, requests)
    local_all = (slot_all % held).reshape(4, requests)
    order = jnp.arange(requests, dtype=jnp.int32)
    earlier = order[None, :] < order[:, None]
    same_owner = owner_all[:, :, None] == owner_all[:, None, :]
    rank_all = jnp.sum(same_owner & earlier[None], axis=2)
    lanes = jnp.arange(held * rank, dtype=jnp.int32)
    fold = (lanes[:, None] % rank == jnp.arange(rank)[None, :]).astype(BF16)
    down_t = jnp.transpose(down, (0, 2, 1)).reshape(held * rank, depth)
    up_2d = up.reshape(held * rank, up.shape[2])
    slots = jnp.arange(capacity, dtype=jnp.int32)
    low, slot_adapter = [], []
    for i in range(4):
        home = s ^ i
        owner = lax.dynamic_index_in_dim(owner_all, home, 0, keepdims=False)
        local = lax.dynamic_index_in_dim(local_all, home, 0, keepdims=False)
        turn = lax.dynamic_index_in_dim(rank_all, home, 0, keepdims=False)
        every = lax.dot_general(xs[i], down_t, (((1,), (1,)), ((), ())), preferred_element_type=F32)
        row_local = jnp.repeat(local, tokens)
        mask = (lanes[None, :] // rank) == row_local[:, None]
        picked = jnp.where(mask, every.astype(BF16), jnp.zeros((), BF16))
        mine = (owner == s)[None, :] & (turn[None, :] == slots[:, None])
        slot_adapter.append(jnp.sum(jnp.where(mine, local[None, :], 0), axis=1))
        choose = mine[:, None, :, None] & (token[None, :, None, None] == token[None, None, None, :])
        choose = choose.reshape(capacity * tokens, rows).astype(BF16)
        folded = jnp.dot(picked, fold, preferred_element_type=F32).astype(BF16)
        low.append(jnp.dot(choose, folded, preferred_element_type=F32).astype(BF16))
    low = jnp.concatenate(
        [jnp.concatenate(low[:2], axis=0), jnp.concatenate(low[2:], axis=0)], axis=1
    )
    total = low.astype(F32)
    for shift in (1, 2, 3):
        total = total + lax.ppermute(low, "tensor", [(i, i ^ shift) for i in range(4)]).astype(F32)
    total = total.astype(BF16)
    total = jnp.concatenate([total[:, :rank], total[:, rank:]], axis=0)
    adapter = jnp.repeat(jnp.concatenate(slot_adapter), tokens)
    spread = jnp.where(
        (lanes[None, :] // rank) == adapter[:, None],
        jnp.tile(total, (1, held)),
        jnp.zeros((), BF16),
    )
    delta = jnp.dot(spread, up_2d, preferred_element_type=F32).astype(BF16)
    size = capacity * tokens
    deltas = [delta[:size]] + [on_store(delta[i * size : (i + 1) * size], i) for i in (1, 2, 3)]

    sums = [starts[i][1] for i in range(4)]
    root_chip = t // 2
    my_key = s ^ (2 * root_chip)
    ahead = sum(jnp.where(((s ^ i) ^ (2 * root_chip)) < my_key, sums[i], 0) for i in range(1, 4))
    delay = jnp.where((t == 0) | (t == 3), 1, 0)
    base_pos = where_rows(starts[0][0], len_me, ahead + delay * span).reshape(rows, 1)
    owner_me = lax.dynamic_index_in_dim(owner_all, s, 0, keepdims=False)
    turn_me = lax.dynamic_index_in_dim(rank_all, s, 0, keepdims=False)
    slot_row = ((owner_me ^ s) * capacity + turn_me) * tokens
    delta_pos = jnp.where(
        token[None, :] < len_me[:, None], slot_row[:, None] + token[None, :], -(1 << 20)
    ).reshape(rows, 1)
    out = finish(base_pos, delta_pos, pieces, deltas)
    return out.reshape(requests, tokens, out.shape[1])


def solution(mesh):
    in_specs = (
        P(("groups", "store"), None, "tensor"),
        P("tensor", "store"),
        P("store", "tensor", None),
        P("store", None, "tensor"),
        P("groups"),
        P("groups"),
        P(("groups", "store")),
    )
    out_specs = P(("groups", "store"), None, "tensor")
    four = mesh.shape["store"] == 4 and mesh.shape["tensor"] == 4
    body = square if four else general
    return jax.shard_map(body, mesh=mesh, in_specs=in_specs, out_specs=out_specs, check_vma=False)
```

```python
import functools
import jax
import jax.numpy as jnp
from jax import lax
from jax.experimental import pallas as pl
from jax.experimental.pallas import tpu as pltpu
from jax.sharding import PartitionSpec as P

VMEM_LIMIT = 52 * 1024 * 1024
SMALL_VMEM = 32 * 1024 * 1024
STREAMS = 2
SPAN = 128
BF16 = jnp.bfloat16
F32 = jnp.float32
LIGHT = pl.CostEstimate(flops=0, bytes_accessed=0, transcendentals=0)


def general(
    attention_input,
    base_projection_weight,
    stored_down_maps,
    stored_up_maps,
    request_adapter_index,
    adapter_store_slot,
    lengths,
):
    requests, seq_len, width_in = attention_input.shape
    owner_grouping = stored_down_maps.shape[0]
    stores = lax.axis_size("store")
    my_index = lax.axis_index("store")
    capacity = (2 * requests + stores - 1) // stores
    partial_value = jnp.einsum(
        "qtk,kd->qtd",
        attention_input,
        lax.all_gather(base_projection_weight, "store", axis=1, tiled=True),
        preferred_element_type=jnp.float32,
    )
    base_out = lax.psum_scatter(
        partial_value.astype(jnp.bfloat16), "tensor", scatter_dimension=2, tiled=True
    ).astype(jnp.float32)
    slot_all = adapter_store_slot[request_adapter_index]
    owner_all = (slot_all // owner_grouping).reshape(stores, requests)
    local_all = (slot_all % owner_grouping).reshape(stores, requests)
    positions = jnp.arange(requests, dtype=jnp.int32)
    earlier = positions[None, :] < positions[:, None]
    same_owner = owner_all[:, :, None] == owner_all[:, None, :]
    rank_all = jnp.sum(same_owner & earlier[None], axis=2)
    owner_mine = lax.dynamic_index_in_dim(owner_all, my_index, 0, keepdims=False)
    rank_mine = lax.dynamic_index_in_dim(rank_all, my_index, 0, keepdims=False)
    owner_range = jnp.arange(stores, dtype=jnp.int32)
    slot_range = jnp.arange(capacity, dtype=jnp.int32)
    local_range = jnp.arange(owner_grouping, dtype=jnp.int32)
    pick_table = (
        (owner_mine[:, None, None] == owner_range[None, :, None])
        & (rank_mine[:, None, None] == slot_range[None, None, :])
    ).astype(jnp.bfloat16)
    selection_matrix = jnp.sum(
        (
            (owner_all == my_index)[:, :, None, None]
            & (rank_all[:, :, None, None] == slot_range[None, None, :, None])
            & (local_all[:, :, None, None] == local_range[None, None, None, :])
        ).astype(jnp.float32),
        axis=1,
    ).astype(jnp.bfloat16)
    outgoing = jnp.einsum(
        "qoc,qtk->octk", pick_table, attention_input, preferred_element_type=jnp.float32
    ).astype(jnp.bfloat16)
    arrived = lax.all_to_all(outgoing, "store", split_axis=0, concat_axis=0, tiled=True)
    down_sel = jnp.einsum(
        "pmb,bwf->pmwf", selection_matrix, stored_down_maps, preferred_element_type=jnp.float32
    ).astype(jnp.bfloat16)
    up_sel = jnp.einsum(
        "ehw,wkx->ehkx", selection_matrix, stored_up_maps, preferred_element_type=jnp.float32
    ).astype(jnp.bfloat16)
    low_part = jnp.einsum("octk,ockr->octr", arrived, down_sel, preferred_element_type=jnp.float32)
    low_full = lax.psum(low_part.astype(jnp.bfloat16), "tensor")
    delta_rows = jnp.einsum(
        "octr,ocrd->octd", low_full, up_sel, preferred_element_type=jnp.float32
    ).astype(jnp.bfloat16)
    returned = lax.all_to_all(delta_rows, "store", split_axis=0, concat_axis=0, tiled=True)
    my_delta = jnp.einsum("qoc,octd->qtd", pick_table, returned, preferred_element_type=jnp.float32)
    token_slots = jnp.arange(seq_len, dtype=jnp.int32)
    valid_mask = (token_slots[None, :] < lengths[:, None]).astype(jnp.float32)
    total = base_out + 2.0 * my_delta
    return (total * valid_mask[:, :, None]).astype(jnp.bfloat16)


def where_am_i(meta_ref):
    s, t = meta_ref[0], meta_ref[1]
    chip = s // 2
    return s, t, chip, jnp.where(chip == 1, t, 3 - t)


def total_of(ref):
    total = ref[0]
    for q in range(1, ref.shape[0]):
        total = total + ref[q]
    return total


def tie_kernel(*refs):
    pass


def after(value, *deps):
    anywhere = pl.BlockSpec(memory_space=pl.ANY)
    return pl.pallas_call(
        tie_kernel,
        in_specs=[anywhere] * (1 + len(deps)),
        out_specs=anywhere,
        out_shape=jax.ShapeDtypeStruct(value.shape, value.dtype),
        input_output_aliases={0: 0},
        cost_estimate=LIGHT,
    )(value, *deps)


def project_kernel(first, blocks, tokens, span, ndeps, *refs):
    meta_ref, len_refs = refs[0], refs[1 : 1 + blocks]
    x_refs, w_ref = refs[1 + blocks : 1 + 2 * blocks], refs[1 + 2 * blocks]
    out_ref, packed = refs[-2], refs[-1]
    rows = packed.shape[0]

    @pl.when(pl.program_id(0) == 0)
    def _():
        s, _, _, u = where_am_i(meta_ref)
        width = x_refs[0].shape[0]
        lead = (s % 2) == 0
        sums = [total_of(r) for r in len_refs]
        starts = [jnp.where(lead, 0, sums[1]), jnp.where(lead, sums[0], 0)]
        if blocks == 4:
            own = sums[0] + sums[1]
            starts += [own + jnp.where(lead, 0, sums[3]), own + jnp.where(lead, sums[2], 0)]
        lane = lax.broadcasted_iota(jnp.int32, (1, width), 1)
        token = lane % tokens
        wanted = lax.broadcasted_iota(jnp.int32, (rows, width), 0)
        picks = []
        for b in range(blocks):
            start = starts[b] + u * span - first
            spot = jnp.full((1, width), -1, jnp.int32)
            for q in range(width // tokens):
                length = len_refs[b][q]
                here = (lane // tokens == q) & (token < length)
                spot = jnp.where(here, start + token, spot)
                start = start + length
            picks.append(jnp.where(spot == wanted, F32(1), F32(0)).astype(BF16))
        pick = jnp.concatenate(picks, axis=1)
        held_rows = jnp.concatenate([r[...] for r in x_refs], axis=0)
        packed[...] = jnp.dot(pick, held_rows, preferred_element_type=F32).astype(BF16)

    out_ref[...] = jnp.dot(packed[...], w_ref[...], preferred_element_type=F32).astype(BF16)


def project(meta, lens, xs, w, first, rows, span, deps=(), tile=512):
    depth, cols = w.shape
    blocks = len(xs)
    block_rows = xs[0].shape[0]
    tokens = block_rows // lens[0].shape[0]
    smem = pl.BlockSpec(memory_space=pltpu.SMEM)
    return pl.pallas_call(
        functools.partial(project_kernel, first, blocks, tokens, span, len(deps)),
        grid=(cols // tile,),
        in_specs=[smem] * (1 + blocks)
        + [pl.BlockSpec((block_rows, depth), lambda j: (0, 0))] * blocks
        + [pl.BlockSpec((depth, tile), lambda j: (0, j))]
        + [pl.BlockSpec(memory_space=pl.ANY)] * len(deps),
        out_specs=pl.BlockSpec((rows, tile), lambda j: (0, j)),
        out_shape=jax.ShapeDtypeStruct((rows, cols), BF16),
        scratch_shapes=[pltpu.VMEM((rows, depth), BF16)],
        compiler_params=pltpu.CompilerParams(vmem_limit_bytes=VMEM_LIMIT),
        cost_estimate=LIGHT,
    )(meta, *lens, *xs, w, *deps)


def visit(meta_ref, req_ref, slot_ref, flip, held, requests, tokens, act):
    s = meta_ref[0]
    home = s ^ flip
    count = jnp.int32(0)
    for q in range(requests):
        slot = slot_ref[req_ref[home * requests + q]]
        local = lax.rem(slot, held)
        mine = lax.div(slot, held) == s
        row = pl.multiple_of(count * tokens, tokens)

        @pl.when(mine)
        def _():
            act(q, row, local)

        count = count + mine.astype(jnp.int32)


def low_kernel(flips, has_before, held, rank, requests, tokens, *refs):
    meta_ref, req_ref, slot_ref = refs[:3]
    x_refs = refs[3 : 3 + len(flips)]
    down_ref = refs[3 + len(flips)]
    before_ref = refs[4 + len(flips)] if has_before else None
    out_ref, gathered, every = refs[-3:]
    size = out_ref.shape[0] // len(flips)
    lanes = held * rank
    gathered[...] = jnp.zeros(gathered.shape, BF16)
    for i, flip in enumerate(flips):

        def collect(q, row, local, i=i):
            gathered[pl.ds(i * size + row, tokens), :] = x_refs[i][q * tokens : (q + 1) * tokens, :]

        visit(meta_ref, req_ref, slot_ref, flip, held, requests, tokens, collect)
    product = lax.dot_general(
        gathered[...], down_ref[...], (((1,), (1,)), ((), ())), preferred_element_type=F32
    )
    gathered[:, :lanes] = product.astype(BF16)
    every[...] = jnp.zeros(every.shape, BF16)
    group = lax.broadcasted_iota(jnp.int32, (1, lanes), 1) // rank
    for i, flip in enumerate(flips):

        def mask(q, row, local, i=i):
            here = pl.ds(i * size + row, tokens)
            value = gathered[here, :lanes].astype(F32)
            every[here, :] = jnp.where(group == local, value, F32(0)).astype(BF16)

        visit(meta_ref, req_ref, slot_ref, flip, held, requests, tokens, mask)
    source = lax.broadcasted_iota(jnp.int32, (lanes, 2 * rank), 0) % rank
    target = lax.broadcasted_iota(jnp.int32, (lanes, 2 * rank), 1)
    shift = rank if before_ref is not None else 0
    fold = jnp.where(source + shift == target, F32(1), F32(0)).astype(BF16)
    result = jnp.dot(every[...], fold, preferred_element_type=F32)
    if before_ref is not None:
        result = result + before_ref[...].astype(F32)
    out_ref[...] = result.astype(BF16)


def low_rank(meta, req, slot, xs, flips, down_t, before, held, rank, tokens, capacity, deps):
    requests = xs[0].shape[0] // tokens
    size = capacity * tokens * len(flips)
    depth = xs[0].shape[1]
    smem = pl.BlockSpec(memory_space=pltpu.SMEM)
    vmem = pl.BlockSpec(memory_space=pltpu.VMEM)
    extra = [] if before is None else [before]
    return pl.pallas_call(
        functools.partial(low_kernel, flips, before is not None, held, rank, requests, tokens),
        in_specs=[smem] * 3 + [vmem] * (len(flips) + 1 + len(extra)) + [pl.BlockSpec(memory_space=pl.ANY)] * len(deps),
        out_specs=vmem,
        out_shape=jax.ShapeDtypeStruct((size, 2 * rank), BF16),
        scratch_shapes=[pltpu.VMEM((size, depth), BF16), pltpu.VMEM((size, held * rank), BF16)],
        compiler_params=pltpu.CompilerParams(vmem_limit_bytes=VMEM_LIMIT),
        cost_estimate=LIGHT,
    )(meta, req, slot, *xs, down_t, *extra, *deps)


def up_kernel(ndeps, held, rank, requests, tokens, meta_ref, req_ref, slot_ref, *refs):
    low_refs, up_ref, out_refs = refs[:4], refs[4], refs[5 + ndeps : 9 + ndeps]
    wide, spread = refs[-2:]
    lanes = held * rank
    half = low_refs[0].shape[0]
    size = half // 2

    @pl.when(pl.program_id(0) == 0)
    def _():
        total = low_refs[0][...].astype(F32)
        for r in low_refs[1:]:
            total = total + r[...].astype(F32)
        total = total.astype(BF16)
        source = lax.broadcasted_iota(jnp.int32, (2 * rank, lanes), 0)
        target = lax.broadcasted_iota(jnp.int32, (2 * rank, lanes), 1) % rank
        for h in range(2):
            tile = jnp.where(source == target + h * rank, F32(1), F32(0)).astype(BF16)
            wide[h * half : (h + 1) * half, :] = jnp.dot(
                total, tile, preferred_element_type=F32
            ).astype(BF16)
        spread[...] = jnp.zeros(spread.shape, BF16)
        group = lax.broadcasted_iota(jnp.int32, (1, lanes), 1) // rank
        for i in range(4):

            def mask(q, row, local, i=i):
                here = pl.ds(i * size + row, tokens)
                value = wide[here, :].astype(F32)
                spread[here, :] = jnp.where(group == local, value, F32(0)).astype(BF16)

            visit(meta_ref, req_ref, slot_ref, i, held, requests, tokens, mask)

    result = jnp.dot(spread[...], up_ref[...], preferred_element_type=F32).astype(BF16)
    for i in range(4):
        out_refs[i][...] = result[i * size : (i + 1) * size, :]


def up_project(meta, req, slot, lows, up_2d, held, rank, tokens, capacity, requests, deps, tile=512):
    cols = up_2d.shape[1]
    size = capacity * tokens
    smem = pl.BlockSpec(memory_space=pltpu.SMEM)
    return pl.pallas_call(
        functools.partial(up_kernel, len(deps), held, rank, requests, tokens),
        grid=(cols // tile,),
        in_specs=[smem] * 3
        + [pl.BlockSpec(lows[0].shape, lambda j: (0, 0))] * 4
        + [pl.BlockSpec((held * rank, tile), lambda j: (0, j))]
        + [pl.BlockSpec(memory_space=pl.ANY)] * len(deps),
        out_specs=[pl.BlockSpec((size, tile), lambda j: (0, j))] * 4,
        out_shape=[jax.ShapeDtypeStruct((size, cols), BF16)] * 4,
        scratch_shapes=[pltpu.VMEM((4 * size, held * rank), BF16)] * 2,
        compiler_params=pltpu.CompilerParams(vmem_limit_bytes=VMEM_LIMIT),
        cost_estimate=LIGHT,
    )(meta, req, slot, *lows, up_2d, *deps)


def finish_kernel(n, sizes, first, span, held, requests, tokens, capacity, with_delta, with_acc, *refs):
    meta_ref, req_ref, slot_ref = refs[:3]
    len_refs = refs[3:7]
    at = 7
    value_refs, got_refs = refs[at : at + n], refs[at + n : at + 2 * n]
    at += 2 * n
    delta_refs = refs[at : at + 4] if with_delta else ()
    at += len(delta_refs)
    acc_ref = refs[at] if with_acc else None
    out_ref, picks, dpicks = refs[-3:]
    s, t, _, _ = where_am_i(meta_ref)
    size = capacity * tokens
    keep = (s == t) | (s == (t ^ 2))

    @pl.when(pl.program_id(0) == 0)
    def _():
        flip = 2 * (t // 2)
        key = s ^ flip
        start = jnp.where((t == 0) | (t == 3), 3, 2) * span - first
        for i in range(1, 4):
            start = start + jnp.where(((s ^ i) ^ flip) < key, total_of(len_refs[i]), 0)
        depth = picks.shape[1]
        token = lax.broadcasted_iota(jnp.int32, (tokens, depth), 0)
        base = lax.broadcasted_iota(jnp.int32, (tokens, depth), 1) - token
        wide = dpicks.shape[1]
        dtoken = lax.broadcasted_iota(jnp.int32, (tokens, wide), 0)
        dbase = lax.broadcasted_iota(jnp.int32, (tokens, wide), 1) - dtoken
        counts = [jnp.int32(0)] * 4
        for q in range(requests):
            length = len_refs[0][q]
            here = (base == start) & (token < length)
            picks[q * tokens : (q + 1) * tokens, :] = jnp.where(here, F32(1), F32(0)).astype(BF16)
            start = start + length
            if with_delta:
                owner = lax.div(slot_ref[req_ref[s * requests + q]], held) ^ s
                turn = jnp.int32(0)
                for i in range(4):
                    turn = turn + jnp.where(owner == i, counts[i], 0)
                    counts[i] = counts[i] + jnp.where(owner == i, 1, 0)
                here = (dbase == owner * size + turn * tokens) & (dtoken < length)
                dpicks[q * tokens : (q + 1) * tokens, :] = jnp.where(here, F32(2), F32(0)).astype(BF16)

    def run(group):
        total = None
        for i, (ref, count) in enumerate(zip(group, sizes)):
            offset = sum(sizes[:i])
            part = jnp.dot(picks[:, offset : offset + count], ref[...], preferred_element_type=F32)
            total = part if total is None else total + part
        if with_delta:
            stack = jnp.concatenate([r[...] for r in delta_refs], axis=0)
            total = total + jnp.dot(dpicks[...], stack, preferred_element_type=F32)
        if with_acc:
            total = total + acc_ref[...]
        out_ref[...] = total.astype(out_ref.dtype)

    @pl.when(keep)
    def _():
        run(value_refs)

    @pl.when(jnp.logical_not(keep))
    def _():
        run(got_refs)


def finish(meta, req, slot, lens, values, gots, first, deltas, acc, out_dtype, span, held, tokens, capacity, tile=512):
    requests = lens[0].shape[0]
    rows = requests * tokens
    cols = values[0].shape[1]
    sizes = [v.shape[0] for v in values]
    depth = sum(sizes)
    wide = 4 * capacity * tokens
    smem = pl.BlockSpec(memory_space=pltpu.SMEM)
    big = list(values) + list(gots) + list(deltas) + ([] if acc is None else [acc])
    return pl.pallas_call(
        functools.partial(
            finish_kernel,
            len(sizes), sizes, first, span, held, requests, tokens, capacity, bool(deltas), acc is not None,
        ),
        grid=(cols // tile,),
        in_specs=[smem] * 7 + [pl.BlockSpec((a.shape[0], tile), lambda j: (0, j)) for a in big],
        out_specs=pl.BlockSpec((rows, tile), lambda j: (0, j)),
        out_shape=jax.ShapeDtypeStruct((rows, cols), out_dtype),
        scratch_shapes=[
            pltpu.VMEM((rows, depth), BF16),
            pltpu.VMEM((rows, wide if deltas else 128), BF16),
        ],
        compiler_params=pltpu.CompilerParams(vmem_limit_bytes=SMALL_VMEM),
        cost_estimate=LIGHT,
    )(meta, req, slot, *lens, *big)


def on_store(value, flip):
    return lax.ppermute(value, "store", [(i, i ^ flip) for i in range(4)])


def plane(s, u):
    return u if s >= 2 else 3 - u


def last_step(s):
    return 3 if s in (0, 3) else 2


def on_mesh(value, pairs):
    return lax.ppermute(value, ("tensor", "store"), [(a * 4 + b, c * 4 + d) for (a, b), (c, d) in pairs])


def square(x, w, down, up, req, slot, lengths):
    requests, tokens, depth = x.shape
    cols = w.shape[1]
    rows = requests * tokens
    live = 3 * rows
    held, _, rank = down.shape
    capacity = requests // 2
    span = SPAN
    steps = live // span
    edge = cols // 2 + 128
    bounds = ((0, edge), (edge, cols))

    s = lax.axis_index("store")
    t = lax.axis_index("tensor")
    meta = jnp.stack([s, t]).astype(jnp.int32)

    x_me = x.reshape(rows, depth)
    x_far = on_store(x_me, 2)
    len_me = lengths
    len_sib = on_store(len_me, 1)
    x_sib = on_store(x_me, 1)
    lens_far = on_store(jnp.concatenate([len_me, len_sib]), 2)
    len_far, len_fsib = lens_far[:requests], lens_far[requests:]
    x_fsib = on_store(x_far, 1)
    lens = [len_me, len_sib, len_far, len_fsib]
    xs = [x_me, x_sib, x_far, x_fsib]
    down_t = jnp.transpose(down, (0, 2, 1)).reshape(held * rank, depth)
    up_2d = up.reshape(held * rank, cols)

    early = rows // span
    back_pairs = [((plane(b, 3), b), (plane(b, 2), b)) for b in (1, 2)]
    across = [((v, v), (v, v ^ 2)) for v in range(4)]
    beside = [((v, v), (v, v ^ 1)) for v in range(4)] + [((v, v ^ 2), (v, v ^ 3)) for v in range(4)]
    is_root = s == t
    chip = s // 2
    u = jnp.where(chip == 1, t, 3 - t)

    final, carry, parts = {}, [None] * STREAMS, {}

    def chunk_of(source, k, j):
        at = jnp.clip(k - u, 0, steps - 1) * span
        lo, hi = bounds[j]
        return lax.dynamic_slice(source, (at, lo), (span, hi - lo))

    def chain_step(k, *deps):
        pairs = [
            ((plane(b, v), b), (plane(b, v + 1), b))
            for b in range(4)
            for v in range(last_step(b))
            if 0 <= k - v < steps
        ]
        for j in range(STREAMS):
            if k < early:
                value = parts[0][k * span : (k + 1) * span, bounds[j][0] : bounds[j][1]]
            elif k == early:
                value = parts[1][:, bounds[j][0] : bounds[j][1]]
            else:
                value = chunk_of(parts[2], k, j)
            if carry[j] is not None:
                came = carry[j]
                if deps and not j:
                    came = after(came, *deps)
                value = (value.astype(F32) + came.astype(F32)).astype(BF16)
            final[k, j] = value
            carry[j] = on_mesh(value, pairs) if pairs else None

    values, gots = [], []

    def post(lo, hi):
        columns = []
        for j in range(STREAMS):
            column = []
            for k in range(lo, hi):
                value = final[k, j]
                if k < steps + 2:
                    value = (value.astype(F32) + chunk_of(back, k, j).astype(F32)).astype(BF16)
                column.append(value)
            columns.append(jnp.concatenate(column, axis=0))
        value = jnp.concatenate(columns, axis=1)
        if (hi - 2) * span > rows:
            value = jnp.where(is_root, value, on_mesh(value, across))
        values.append(value)
        gots.append(on_mesh(value, beside))

    parts[0] = project(meta, lens[:2], xs[:2], w, 0, early * span, span)
    chain_step(0)
    low = low_rank(
        meta, req, slot, xs[:2], (0, 1), down_t, None, held, rank, tokens, capacity, (parts[0],)
    )
    chain_step(1)
    x_far = after(x_far, final[1, 0], final[1, 1], low)
    x_fsib = on_store(x_far, 1)
    xs = [x_me, x_sib, x_far, x_fsib]
    parts[1] = project(meta, lens, xs, w, early * span, span, span)
    chain_step(2)
    parts[2] = project(meta, lens, xs, w, 0, live, 0, (final[2, 0], final[2, 1]))
    chain_step(3)
    back = on_mesh(parts[2], back_pairs)
    low = low_rank(
        meta, req, slot, xs[2:], (2, 3), down_t, low, held, rank, tokens, capacity, (final[3, 0], final[3, 1])
    )
    lows = [low] + [lax.ppermute(low, "tensor", [(i, i ^ f) for i in range(4)]) for f in (1, 2, 3)]
    chain_step(4, low)
    delta = up_project(meta, req, slot, lows, up_2d, held, rank, tokens, capacity, requests, (final[4, 0], final[4, 1]))
    deltas = [delta[0]] + [on_store(delta[i], i) for i in (1, 2, 3)]
    chain_step(5, delta[0])
    back = after(back, final[5, 0], final[5, 1])
    post(2, 4)
    chain_step(6)
    post(4, 6)
    chain_step(7)
    partial = finish(
        meta, req, slot, lens, values[:1], gots[:1], 2 * span, deltas, None, F32, span, held, tokens, capacity
    )
    chain_step(8, partial)
    post(6, 8)
    post(8, 9)
    out = finish(
        meta, req, slot, lens, values[1:], gots[1:], 4 * span, (), partial, BF16, span, held, tokens, capacity
    )
    return out.reshape(requests, tokens, cols)


def solution(mesh):
    in_specs = (
        P(("groups", "store"), None, "tensor"),
        P("tensor", "store"),
        P("store", "tensor", None),
        P("store", None, "tensor"),
        P("groups"),
        P("groups"),
        P(("groups", "store")),
    )
    out_specs = P(("groups", "store"), None, "tensor")
    four = mesh.shape["store"] == 4 and mesh.shape["tensor"] == 4
    body = square if four else general
    return jax.shard_map(body, mesh=mesh, in_specs=in_specs, out_specs=out_specs, check_vma=False)
```

```python
import functools
import jax
import jax.numpy as jnp
from jax import lax
from jax.experimental import pallas as pl
from jax.experimental.pallas import tpu as pltpu
from jax.sharding import PartitionSpec as P

VMEM_LIMIT = 52 * 1024 * 1024
SMALL_VMEM = 32 * 1024 * 1024
STREAMS = 2
SPAN = 128
SLOTS = 16
BF16 = jnp.bfloat16
F32 = jnp.float32
LIGHT = pl.CostEstimate(flops=0, bytes_accessed=0, transcendentals=0)


def general(
    attention_input,
    base_projection_weight,
    stored_down_maps,
    stored_up_maps,
    request_adapter_index,
    adapter_store_slot,
    lengths,
):
    requests, seq_len, width_in = attention_input.shape
    owner_grouping = stored_down_maps.shape[0]
    stores = lax.axis_size("store")
    my_index = lax.axis_index("store")
    capacity = (2 * requests + stores - 1) // stores
    partial_value = jnp.einsum(
        "qtk,kd->qtd",
        attention_input,
        lax.all_gather(base_projection_weight, "store", axis=1, tiled=True),
        preferred_element_type=jnp.float32,
    )
    base_out = lax.psum_scatter(
        partial_value.astype(jnp.bfloat16), "tensor", scatter_dimension=2, tiled=True
    ).astype(jnp.float32)
    slot_all = adapter_store_slot[request_adapter_index]
    owner_all = (slot_all // owner_grouping).reshape(stores, requests)
    local_all = (slot_all % owner_grouping).reshape(stores, requests)
    positions = jnp.arange(requests, dtype=jnp.int32)
    earlier = positions[None, :] < positions[:, None]
    same_owner = owner_all[:, :, None] == owner_all[:, None, :]
    rank_all = jnp.sum(same_owner & earlier[None], axis=2)
    owner_mine = lax.dynamic_index_in_dim(owner_all, my_index, 0, keepdims=False)
    rank_mine = lax.dynamic_index_in_dim(rank_all, my_index, 0, keepdims=False)
    owner_range = jnp.arange(stores, dtype=jnp.int32)
    slot_range = jnp.arange(capacity, dtype=jnp.int32)
    local_range = jnp.arange(owner_grouping, dtype=jnp.int32)
    pick_table = (
        (owner_mine[:, None, None] == owner_range[None, :, None])
        & (rank_mine[:, None, None] == slot_range[None, None, :])
    ).astype(jnp.bfloat16)
    selection_matrix = jnp.sum(
        (
            (owner_all == my_index)[:, :, None, None]
            & (rank_all[:, :, None, None] == slot_range[None, None, :, None])
            & (local_all[:, :, None, None] == local_range[None, None, None, :])
        ).astype(jnp.float32),
        axis=1,
    ).astype(jnp.bfloat16)
    outgoing = jnp.einsum(
        "qoc,qtk->octk", pick_table, attention_input, preferred_element_type=jnp.float32
    ).astype(jnp.bfloat16)
    arrived = lax.all_to_all(outgoing, "store", split_axis=0, concat_axis=0, tiled=True)
    down_sel = jnp.einsum(
        "pmb,bwf->pmwf", selection_matrix, stored_down_maps, preferred_element_type=jnp.float32
    ).astype(jnp.bfloat16)
    up_sel = jnp.einsum(
        "ehw,wkx->ehkx", selection_matrix, stored_up_maps, preferred_element_type=jnp.float32
    ).astype(jnp.bfloat16)
    low_part = jnp.einsum("octk,ockr->octr", arrived, down_sel, preferred_element_type=jnp.float32)
    low_full = lax.psum(low_part.astype(jnp.bfloat16), "tensor")
    delta_rows = jnp.einsum(
        "octr,ocrd->octd", low_full, up_sel, preferred_element_type=jnp.float32
    ).astype(jnp.bfloat16)
    returned = lax.all_to_all(delta_rows, "store", split_axis=0, concat_axis=0, tiled=True)
    my_delta = jnp.einsum("qoc,octd->qtd", pick_table, returned, preferred_element_type=jnp.float32)
    token_slots = jnp.arange(seq_len, dtype=jnp.int32)
    valid_mask = (token_slots[None, :] < lengths[:, None]).astype(jnp.float32)
    total = base_out + 2.0 * my_delta
    return (total * valid_mask[:, :, None]).astype(jnp.bfloat16)


def where_am_i(meta_ref):
    s, t = meta_ref[0], meta_ref[1]
    chip = s // 2
    return s, t, chip, jnp.where(chip == 1, t, 3 - t)


def total_of(ref):
    total = ref[0]
    for q in range(1, ref.shape[0]):
        total = total + ref[q]
    return total


def tie_kernel(*refs):
    pass


def after(value, *deps):
    anywhere = pl.BlockSpec(memory_space=pl.ANY)
    return pl.pallas_call(
        tie_kernel,
        in_specs=[anywhere] * (1 + len(deps)),
        out_specs=anywhere,
        out_shape=jax.ShapeDtypeStruct(value.shape, value.dtype),
        input_output_aliases={0: 0},
        cost_estimate=LIGHT,
    )(value, *deps)


def project_kernel(first, blocks, block_rows, tokens, span, *refs):
    meta_ref, len_refs = refs[0], refs[1 : 1 + blocks]
    x_refs, w_ref = refs[1 + blocks : 1 + 2 * blocks], refs[1 + 2 * blocks]
    out_ref, packed = refs[-2], refs[-1]
    rows = packed.shape[0]

    @pl.when(pl.program_id(0) == 0)
    def _():
        s, _, _, u = where_am_i(meta_ref)
        width = block_rows
        lead = (s % 2) == 0
        sums = [total_of(r) for r in len_refs]
        starts = [jnp.where(lead, 0, sums[1]), jnp.where(lead, sums[0], 0)]
        if blocks == 4:
            own = sums[0] + sums[1]
            starts += [own + jnp.where(lead, 0, sums[3]), own + jnp.where(lead, sums[2], 0)]
        lane = lax.broadcasted_iota(jnp.int32, (1, width), 1)
        token = lane % tokens
        wanted = lax.broadcasted_iota(jnp.int32, (rows, width), 0)
        picks = []
        for b in range(blocks):
            start = starts[b] + u * span - first
            spot = jnp.full((1, width), -1, jnp.int32)
            for q in range(width // tokens):
                length = len_refs[b][q]
                here = (lane // tokens == q) & (token < length)
                spot = jnp.where(here, start + token, spot)
                start = start + length
            picks.append(jnp.where(spot == wanted, F32(1), F32(0)).astype(BF16))
        pick = jnp.concatenate(picks, axis=1)
        held_rows = jnp.concatenate([r[...] for r in x_refs], axis=0)
        packed[...] = jnp.dot(pick, held_rows, preferred_element_type=F32).astype(BF16)

    out_ref[...] = jnp.dot(packed[...], w_ref[...], preferred_element_type=F32).astype(BF16)


def project(meta, lens, xs, w, first, rows, span, deps=(), tile=512):
    depth, cols = w.shape
    blocks = len(xs)
    block_rows = lens[0].shape[0] * SLOTS
    tokens = SLOTS
    smem = pl.BlockSpec(memory_space=pltpu.SMEM)
    return pl.pallas_call(
        functools.partial(project_kernel, first, blocks, block_rows, tokens, span),
        grid=(cols // tile,),
        in_specs=[smem] * (1 + blocks)
        + [pl.BlockSpec((block_rows, depth), lambda j: (0, 0))] * blocks
        + [pl.BlockSpec((depth, tile), lambda j: (0, j))]
        + [pl.BlockSpec(memory_space=pl.ANY)] * len(deps),
        out_specs=pl.BlockSpec((rows, tile), lambda j: (0, j)),
        out_shape=jax.ShapeDtypeStruct((rows, cols), BF16),
        scratch_shapes=[pltpu.VMEM((rows, depth), BF16)],
        compiler_params=pltpu.CompilerParams(vmem_limit_bytes=VMEM_LIMIT),
        cost_estimate=LIGHT,
    )(meta, *lens, *xs, w, *deps)


def visit(meta_ref, req_ref, slot_ref, flip, held, requests, tokens, act):
    s = meta_ref[0]
    home = s ^ flip
    count = jnp.int32(0)
    for q in range(requests):
        slot = slot_ref[req_ref[home * requests + q]]
        local = lax.rem(slot, held)
        mine = lax.div(slot, held) == s
        row = pl.multiple_of(count * tokens, tokens)

        @pl.when(mine)
        def _():
            act(q, row, local)

        count = count + mine.astype(jnp.int32)


def low_kernel(flips, has_before, held, rank, requests, tokens, *refs):
    meta_ref, req_ref, slot_ref = refs[:3]
    x_refs = refs[3 : 3 + len(flips)]
    down_ref = refs[3 + len(flips)]
    before_ref = refs[4 + len(flips)] if has_before else None
    out_ref, gathered, every = refs[-3:]
    size = out_ref.shape[0] // len(flips)
    lanes = held * rank
    gathered[...] = jnp.zeros(gathered.shape, BF16)
    for i, flip in enumerate(flips):

        def collect(q, row, local, i=i):
            gathered[pl.ds(i * size + row, tokens), :] = x_refs[i][q * tokens : (q + 1) * tokens, :]

        visit(meta_ref, req_ref, slot_ref, flip, held, requests, tokens, collect)
    product = lax.dot_general(
        gathered[...], down_ref[...], (((1,), (1,)), ((), ())), preferred_element_type=F32
    )
    gathered[:, :lanes] = product.astype(BF16)
    every[...] = jnp.zeros(every.shape, BF16)
    group = lax.broadcasted_iota(jnp.int32, (1, lanes), 1) // rank
    for i, flip in enumerate(flips):

        def mask(q, row, local, i=i):
            here = pl.ds(i * size + row, tokens)
            value = gathered[here, :lanes].astype(F32)
            every[here, :] = jnp.where(group == local, value, F32(0)).astype(BF16)

        visit(meta_ref, req_ref, slot_ref, flip, held, requests, tokens, mask)
    source = lax.broadcasted_iota(jnp.int32, (lanes, 2 * rank), 0) % rank
    target = lax.broadcasted_iota(jnp.int32, (lanes, 2 * rank), 1)
    shift = rank if before_ref is not None else 0
    fold = jnp.where(source + shift == target, F32(1), F32(0)).astype(BF16)
    result = jnp.dot(every[...], fold, preferred_element_type=F32)
    if before_ref is not None:
        result = result + before_ref[...].astype(F32)
    out_ref[...] = result.astype(BF16)


def low_rank(meta, req, slot, xs, flips, down_t, before, held, rank, tokens, capacity, deps):
    requests = 2 * capacity
    size = capacity * tokens * len(flips)
    depth = xs[0].shape[1]
    smem = pl.BlockSpec(memory_space=pltpu.SMEM)
    vmem = pl.BlockSpec(memory_space=pltpu.VMEM)
    extra = [] if before is None else [before]
    return pl.pallas_call(
        functools.partial(low_kernel, flips, before is not None, held, rank, requests, tokens),
        in_specs=[smem] * 3 + [vmem] * (len(flips) + 1 + len(extra)) + [pl.BlockSpec(memory_space=pl.ANY)] * len(deps),
        out_specs=vmem,
        out_shape=jax.ShapeDtypeStruct((size, 2 * rank), BF16),
        scratch_shapes=[pltpu.VMEM((size, depth), BF16), pltpu.VMEM((size, held * rank), BF16)],
        compiler_params=pltpu.CompilerParams(vmem_limit_bytes=VMEM_LIMIT),
        cost_estimate=LIGHT,
    )(meta, req, slot, *xs, down_t, *extra, *deps)


def up_kernel(ndeps, held, rank, requests, tokens, meta_ref, req_ref, slot_ref, *refs):
    low_refs, up_ref, out_refs = refs[:4], refs[4], refs[5 + ndeps : 9 + ndeps]
    wide, spread = refs[-2:]
    lanes = held * rank
    half = low_refs[0].shape[0]
    size = half // 2

    @pl.when(pl.program_id(0) == 0)
    def _():
        total = low_refs[0][...].astype(F32)
        for r in low_refs[1:]:
            total = total + r[...].astype(F32)
        total = total.astype(BF16)
        source = lax.broadcasted_iota(jnp.int32, (2 * rank, lanes), 0)
        target = lax.broadcasted_iota(jnp.int32, (2 * rank, lanes), 1) % rank
        for h in range(2):
            tile = jnp.where(source == target + h * rank, F32(1), F32(0)).astype(BF16)
            wide[h * half : (h + 1) * half, :] = jnp.dot(
                total, tile, preferred_element_type=F32
            ).astype(BF16)
        spread[...] = jnp.zeros(spread.shape, BF16)
        group = lax.broadcasted_iota(jnp.int32, (1, lanes), 1) // rank
        for i in range(4):

            def mask(q, row, local, i=i):
                here = pl.ds(i * size + row, tokens)
                value = wide[here, :].astype(F32)
                spread[here, :] = jnp.where(group == local, value, F32(0)).astype(BF16)

            visit(meta_ref, req_ref, slot_ref, i, held, requests, tokens, mask)

    result = jnp.dot(spread[...], up_ref[...], preferred_element_type=F32).astype(BF16)
    for i in range(4):
        out_refs[i][...] = result[i * size : (i + 1) * size, :]


def up_project(meta, req, slot, lows, up_2d, held, rank, tokens, capacity, requests, deps, tile=512):
    cols = up_2d.shape[1]
    size = capacity * tokens
    smem = pl.BlockSpec(memory_space=pltpu.SMEM)
    return pl.pallas_call(
        functools.partial(up_kernel, len(deps), held, rank, requests, tokens),
        grid=(cols // tile,),
        in_specs=[smem] * 3
        + [pl.BlockSpec(lows[0].shape, lambda j: (0, 0))] * 4
        + [pl.BlockSpec((held * rank, tile), lambda j: (0, j))]
        + [pl.BlockSpec(memory_space=pl.ANY)] * len(deps),
        out_specs=[pl.BlockSpec((size, tile), lambda j: (0, j))] * 4,
        out_shape=[jax.ShapeDtypeStruct((size, cols), BF16)] * 4,
        scratch_shapes=[pltpu.VMEM((4 * size, held * rank), BF16)] * 2,
        compiler_params=pltpu.CompilerParams(vmem_limit_bytes=VMEM_LIMIT),
        cost_estimate=LIGHT,
    )(meta, req, slot, *lows, up_2d, *deps)


def extend_kernel(len_ref, x_ref, out_ref):
    rows, depth = x_ref.shape
    extra = out_ref.shape[0] - rows
    out_ref[:rows, :] = x_ref[...]
    lane = lax.broadcasted_iota(jnp.int32, (extra, depth), 1)
    below = jnp.zeros((extra, depth), F32)
    for q in range(len_ref.shape[0]):
        below = jnp.where(lane == q, len_ref[q].astype(F32), below)
    out_ref[rows:, :] = below.astype(BF16)


def extend(lengths, x, extra):
    vmem = pl.BlockSpec(memory_space=pltpu.VMEM)
    return pl.pallas_call(
        extend_kernel,
        in_specs=[pl.BlockSpec(memory_space=pltpu.SMEM), vmem],
        out_specs=vmem,
        out_shape=jax.ShapeDtypeStruct((x.shape[0] + extra, x.shape[1]), BF16),
        compiler_params=pltpu.CompilerParams(vmem_limit_bytes=SMALL_VMEM),
        cost_estimate=LIGHT,
    )(lengths, x)


def merge_kernel(count, streams, has_back, u_ref, *refs):
    out_ref = refs[-1]
    span = refs[0].shape[0]
    for i in range(count):
        at = 0
        for j in range(streams):
            piece = refs[i * streams + j]
            value = piece[...]
            width = piece.shape[1]
            if has_back:
                back = refs[count * streams + i][:, at : at + width]
                value = (value.astype(F32) + back.astype(F32)).astype(BF16)
            out_ref[i * span : (i + 1) * span, at : at + width] = value
            at += width


def merge(u, pieces, backs, steps_of):
    count, streams = len(steps_of), len(pieces) // len(steps_of)
    span = pieces[0].shape[0]
    cols = sum(p.shape[1] for p in pieces[:streams])

    def spec_of(low, high, k):
        return pl.BlockSpec((span, cols), lambda i, r: (jnp.clip(k - r[0], low, high) - low, 0))

    specs = [pl.BlockSpec(p.shape, lambda i, r: (0, 0)) for p in pieces]
    specs += [spec_of(low, high, k) for k, (_, low, high) in zip(steps_of, backs)]
    return pl.pallas_call(
        functools.partial(merge_kernel, count, streams, bool(backs)),
        grid_spec=pltpu.PrefetchScalarGridSpec(
            num_scalar_prefetch=1,
            grid=(1,),
            in_specs=specs,
            out_specs=pl.BlockSpec((count * span, cols), lambda i, r: (0, 0)),
        ),
        out_shape=jax.ShapeDtypeStruct((count * span, cols), BF16),
        compiler_params=pltpu.CompilerParams(vmem_limit_bytes=SMALL_VMEM),
        cost_estimate=LIGHT,
    )(u, *pieces, *[b[0] for b in backs])


def finish_kernel(n, sizes, first, span, held, requests, tokens, capacity, with_delta, with_acc, *refs):
    meta_ref, req_ref, slot_ref = refs[:3]
    len_refs = refs[3:7]
    at = 7
    value_refs, got_refs = refs[at : at + n], refs[at + n : at + 2 * n]
    at += 2 * n
    delta_refs = refs[at : at + 4] if with_delta else ()
    at += len(delta_refs)
    acc_ref = refs[at] if with_acc else None
    out_ref, picks, dpicks = refs[-3:]
    s, t, _, _ = where_am_i(meta_ref)
    size = capacity * tokens
    keep = (s == t) | (s == (t ^ 2))

    @pl.when(pl.program_id(0) == 0)
    def _():
        flip = 2 * (t // 2)
        key = s ^ flip
        start = jnp.where((t == 0) | (t == 3), 3, 2) * span - first
        for i in range(1, 4):
            start = start + jnp.where(((s ^ i) ^ flip) < key, total_of(len_refs[i]), 0)
        depth = picks.shape[1]
        token = lax.broadcasted_iota(jnp.int32, (tokens, depth), 0)
        base = lax.broadcasted_iota(jnp.int32, (tokens, depth), 1) - token
        wide = dpicks.shape[1]
        dtoken = lax.broadcasted_iota(jnp.int32, (tokens, wide), 0)
        dbase = lax.broadcasted_iota(jnp.int32, (tokens, wide), 1) - dtoken
        counts = [jnp.int32(0)] * 4
        for q in range(requests):
            length = len_refs[0][q]
            here = (base == start) & (token < length)
            picks[q * tokens : (q + 1) * tokens, :] = jnp.where(here, F32(1), F32(0)).astype(BF16)
            start = start + length
            if with_delta:
                owner = lax.div(slot_ref[req_ref[s * requests + q]], held) ^ s
                turn = jnp.int32(0)
                for i in range(4):
                    turn = turn + jnp.where(owner == i, counts[i], 0)
                    counts[i] = counts[i] + jnp.where(owner == i, 1, 0)
                here = (dbase == owner * size + turn * tokens) & (dtoken < length)
                dpicks[q * tokens : (q + 1) * tokens, :] = jnp.where(here, F32(2), F32(0)).astype(BF16)

    def run(group):
        total = None
        for i, (ref, count) in enumerate(zip(group, sizes)):
            offset = sum(sizes[:i])
            part = jnp.dot(picks[:, offset : offset + count], ref[...], preferred_element_type=F32)
            total = part if total is None else total + part
        if with_delta:
            stack = jnp.concatenate([r[...] for r in delta_refs], axis=0)
            total = total + jnp.dot(dpicks[...], stack, preferred_element_type=F32)
        if with_acc:
            total = total + acc_ref[...]
        out_ref[...] = total.astype(out_ref.dtype)

    @pl.when(keep)
    def _():
        run(value_refs)

    @pl.when(jnp.logical_not(keep))
    def _():
        run(got_refs)


def finish(meta, req, slot, lens, values, gots, first, deltas, acc, out_dtype, span, held, tokens, capacity, deps=(), tile=512):
    requests = lens[0].shape[0]
    rows = requests * tokens
    cols = values[0].shape[1]
    sizes = [v.shape[0] for v in values]
    depth = sum(sizes)
    wide = 4 * capacity * tokens
    smem = pl.BlockSpec(memory_space=pltpu.SMEM)
    big = list(values) + list(gots) + list(deltas) + ([] if acc is None else [acc])
    return pl.pallas_call(
        functools.partial(
            finish_kernel,
            len(sizes), sizes, first, span, held, requests, tokens, capacity, bool(deltas), acc is not None,
        ),
        grid=(cols // tile,),
        in_specs=[smem] * 7
        + [pl.BlockSpec((a.shape[0], tile), lambda j: (0, j)) for a in big]
        + [pl.BlockSpec(memory_space=pl.ANY)] * len(deps),
        out_specs=pl.BlockSpec((rows, tile), lambda j: (0, j)),
        out_shape=jax.ShapeDtypeStruct((rows, cols), out_dtype),
        scratch_shapes=[
            pltpu.VMEM((rows, depth), BF16),
            pltpu.VMEM((rows, wide if deltas else 128), BF16),
        ],
        compiler_params=pltpu.CompilerParams(vmem_limit_bytes=SMALL_VMEM),
        cost_estimate=LIGHT,
    )(meta, req, slot, *lens, *big, *deps)


def on_store(value, flip):
    return lax.ppermute(value, "store", [(i, i ^ flip) for i in range(4)])


def plane(s, u):
    return u if s >= 2 else 3 - u


def last_step(s):
    return 3 if s in (0, 3) else 2


def on_mesh(value, pairs):
    return lax.ppermute(value, ("tensor", "store"), [(a * 4 + b, c * 4 + d) for (a, b), (c, d) in pairs])


def square(x, w, down, up, req, slot, lengths):
    requests, tokens, depth = x.shape
    cols = w.shape[1]
    rows = requests * tokens
    live = 3 * rows
    held, _, rank = down.shape
    capacity = requests // 2
    span = SPAN
    steps = live // span
    edge = cols // 2 + 128
    bounds = ((0, edge), (edge, cols))

    s = lax.axis_index("store")
    t = lax.axis_index("tensor")
    meta = jnp.stack([s, t]).astype(jnp.int32)

    x_me = x.reshape(rows, depth)
    x_out = extend(lengths, x_me, tokens)
    x_far = on_store(x_out, 2)
    x_sib = on_store(x_out, 1)

    def lengths_of(array):
        return array[rows, :requests].astype(jnp.int32)

    lens = [lengths, lengths_of(x_sib)]
    xs = [x_me, x_sib]
    down_t = jnp.transpose(down, (0, 2, 1)).reshape(held * rank, depth)
    up_2d = up.reshape(held * rank, cols)

    early = rows // span
    back_pairs = [((plane(b, 3), b), (plane(b, 2), b)) for b in (1, 2)]
    across = [((v, v), (v, v ^ 2)) for v in range(4)]
    beside = [((v, v), (v, v ^ 1)) for v in range(4)] + [((v, v ^ 2), (v, v ^ 3)) for v in range(4)]
    is_root = s == t
    chip = s // 2
    u = jnp.where(chip == 1, t, 3 - t)

    final, carry, parts = {}, [None] * STREAMS, {}

    def chunk_of(source, k, j):
        at = jnp.clip(k - u, 0, steps - 1) * span
        lo, hi = bounds[j]
        return lax.dynamic_slice(source, (at, lo), (span, hi - lo))

    def chain_step(k, *deps):
        pairs = [
            ((plane(b, v), b), (plane(b, v + 1), b))
            for b in range(4)
            for v in range(last_step(b))
            if 0 <= k - v < steps
        ]
        for j in range(STREAMS):
            if k < early:
                value = parts[0][k * span : (k + 1) * span, bounds[j][0] : bounds[j][1]]
            else:
                value = chunk_of(parts[1], k, j)
            if carry[j] is not None:
                came = carry[j]
                if deps and not j:
                    came = after(came, *deps)
                total = value.astype(F32) + came.astype(F32)
                value = total.astype(BF16)
            final[k, j] = value
            carry[j] = on_mesh(value, pairs) if pairs else None

    values, gots = [], []

    def merged(lo, hi):
        ks = range(lo, hi)
        backs = []
        if hi <= steps + 2:
            for k in ks:
                backs.append(next(b for b in back if b[1] <= k - 2 <= b[2]))
        return merge(u_vec, [final[k, j] for k in ks for j in range(STREAMS)], backs, ks)

    def cross(value):
        return jnp.where(is_root, value, on_mesh(value, across))

    def hand_on(value):
        values.append(value)
        gots.append(on_mesh(value, beside))

    u_vec = u.astype(jnp.int32).reshape(1)
    parts[0] = project(meta, lens[:2], xs[:2], w, 0, early * span, span)
    chain_step(0)
    low = low_rank(
        meta, req, slot, xs[:2], (0, 1), down_t, None, held, rank, tokens, capacity, (parts[0],)
    )
    chain_step(1)
    x_far = after(x_far, final[1, 0], final[1, 1], low)
    x_fsib = on_store(x_far, 1)
    xs = [x_me, x_sib, x_far, x_fsib]
    lens = lens + [lengths_of(x_far), lengths_of(x_fsib)]
    low = low_rank(meta, req, slot, xs[2:], (2, 3), down_t, low, held, rank, tokens, capacity, ())
    lows = [low] + [lax.ppermute(low, "tensor", [(i, i ^ f) for i in range(4)]) for f in (1, 2, 3)]
    parts[1] = project(meta, lens, xs, w, 0, live, 0, (low,))
    chain_step(2)
    delta = up_project(
        meta, req, slot, lows, up_2d, held, rank, tokens, capacity, requests, (final[2, 0], final[2, 1])
    )
    deltas = [delta[0]] + [on_store(delta[i], i) for i in (1, 2, 3)]
    chain_step(3, delta[0])
    cut = steps // 2

    def send_back(low, high, *deps):
        rows_of = after(parts[1][low * span : (high + 1) * span], *deps)
        return on_mesh(rows_of, back_pairs), low, high

    back = [send_back(0, cut - 1, final[3, 0], final[3, 1])]
    chain_step(4, deltas[1])
    back.append(send_back(cut, steps - 1, final[4, 0], final[4, 1]))
    chain_step(5, deltas[2])
    chain_step(6, deltas[3])
    one = merged(2, 4)
    two = merged(4, 6)
    chain_step(7, two)
    hand_on(one)
    two = cross(two)
    three = merged(6, 8)
    chain_step(8, two)
    hand_on(two)
    hand_on(cross(three))
    partial = finish(
        meta, req, slot, lens, values[:1], gots[:1], 2 * span, deltas, None, F32, span, held, tokens, capacity,
        (final[8, 0], final[8, 1]),
    )
    hand_on(cross(merged(8, 9)))
    out = finish(
        meta, req, slot, lens, values[1:], gots[1:], 4 * span, (), partial, BF16, span, held, tokens, capacity
    )
    return out.reshape(requests, tokens, cols)


def solution(mesh):
    in_specs = (
        P(("groups", "store"), None, "tensor"),
        P("tensor", "store"),
        P("store", "tensor", None),
        P("store", None, "tensor"),
        P("groups"),
        P("groups"),
        P(("groups", "store")),
    )
    out_specs = P(("groups", "store"), None, "tensor")
    four = mesh.shape["store"] == 4 and mesh.shape["tensor"] == 4
    body = square if four else general
    return jax.shard_map(body, mesh=mesh, in_specs=in_specs, out_specs=out_specs, check_vma=False)
```

```python
import functools
import jax
import jax.numpy as jnp
from jax import lax
from jax.experimental import pallas as pl
from jax.experimental.pallas import tpu as pltpu
from jax.sharding import PartitionSpec as P

VMEM_LIMIT = 52 * 1024 * 1024
SMALL_VMEM = 32 * 1024 * 1024
STREAMS = 2
SPAN = 128
SLOTS = 16
BF16 = jnp.bfloat16
F32 = jnp.float32
LIGHT = pl.CostEstimate(flops=0, bytes_accessed=0, transcendentals=0)


def general(
    attention_input,
    base_projection_weight,
    stored_down_maps,
    stored_up_maps,
    request_adapter_index,
    adapter_store_slot,
    lengths,
):
    requests, seq_len, width_in = attention_input.shape
    owner_grouping = stored_down_maps.shape[0]
    stores = lax.axis_size("store")
    my_index = lax.axis_index("store")
    capacity = (2 * requests + stores - 1) // stores
    partial_value = jnp.einsum(
        "qtk,kd->qtd",
        attention_input,
        lax.all_gather(base_projection_weight, "store", axis=1, tiled=True),
        preferred_element_type=jnp.float32,
    )
    base_out = lax.psum_scatter(
        partial_value.astype(jnp.bfloat16), "tensor", scatter_dimension=2, tiled=True
    ).astype(jnp.float32)
    slot_all = adapter_store_slot[request_adapter_index]
    owner_all = (slot_all // owner_grouping).reshape(stores, requests)
    local_all = (slot_all % owner_grouping).reshape(stores, requests)
    positions = jnp.arange(requests, dtype=jnp.int32)
    earlier = positions[None, :] < positions[:, None]
    same_owner = owner_all[:, :, None] == owner_all[:, None, :]
    rank_all = jnp.sum(same_owner & earlier[None], axis=2)
    owner_mine = lax.dynamic_index_in_dim(owner_all, my_index, 0, keepdims=False)
    rank_mine = lax.dynamic_index_in_dim(rank_all, my_index, 0, keepdims=False)
    owner_range = jnp.arange(stores, dtype=jnp.int32)
    slot_range = jnp.arange(capacity, dtype=jnp.int32)
    local_range = jnp.arange(owner_grouping, dtype=jnp.int32)
    pick_table = (
        (owner_mine[:, None, None] == owner_range[None, :, None])
        & (rank_mine[:, None, None] == slot_range[None, None, :])
    ).astype(jnp.bfloat16)
    selection_matrix = jnp.sum(
        (
            (owner_all == my_index)[:, :, None, None]
            & (rank_all[:, :, None, None] == slot_range[None, None, :, None])
            & (local_all[:, :, None, None] == local_range[None, None, None, :])
        ).astype(jnp.float32),
        axis=1,
    ).astype(jnp.bfloat16)
    outgoing = jnp.einsum(
        "qoc,qtk->octk", pick_table, attention_input, preferred_element_type=jnp.float32
    ).astype(jnp.bfloat16)
    arrived = lax.all_to_all(outgoing, "store", split_axis=0, concat_axis=0, tiled=True)
    down_sel = jnp.einsum(
        "pmb,bwf->pmwf", selection_matrix, stored_down_maps, preferred_element_type=jnp.float32
    ).astype(jnp.bfloat16)
    up_sel = jnp.einsum(
        "ehw,wkx->ehkx", selection_matrix, stored_up_maps, preferred_element_type=jnp.float32
    ).astype(jnp.bfloat16)
    low_part = jnp.einsum("octk,ockr->octr", arrived, down_sel, preferred_element_type=jnp.float32)
    low_full = lax.psum(low_part.astype(jnp.bfloat16), "tensor")
    delta_rows = jnp.einsum(
        "octr,ocrd->octd", low_full, up_sel, preferred_element_type=jnp.float32
    ).astype(jnp.bfloat16)
    returned = lax.all_to_all(delta_rows, "store", split_axis=0, concat_axis=0, tiled=True)
    my_delta = jnp.einsum("qoc,octd->qtd", pick_table, returned, preferred_element_type=jnp.float32)
    token_slots = jnp.arange(seq_len, dtype=jnp.int32)
    valid_mask = (token_slots[None, :] < lengths[:, None]).astype(jnp.float32)
    total = base_out + 2.0 * my_delta
    return (total * valid_mask[:, :, None]).astype(jnp.bfloat16)


def where_am_i(meta_ref):
    s, t = meta_ref[0], meta_ref[1]
    chip = s // 2
    return s, t, chip, jnp.where(chip == 1, t, 3 - t)


def total_of(ref):
    total = ref[0]
    for q in range(1, ref.shape[0]):
        total = total + ref[q]
    return total


def tie_kernel(*refs):
    pass


def after(value, *deps):
    anywhere = pl.BlockSpec(memory_space=pl.ANY)
    return pl.pallas_call(
        tie_kernel,
        in_specs=[anywhere] * (1 + len(deps)),
        out_specs=anywhere,
        out_shape=jax.ShapeDtypeStruct(value.shape, value.dtype),
        input_output_aliases={0: 0},
        cost_estimate=LIGHT,
    )(value, *deps)


def project_kernel(first, blocks, block_rows, tokens, span, *refs):
    meta_ref, len_refs = refs[0], refs[1 : 1 + blocks]
    x_refs, w_ref = refs[1 + blocks : 1 + 2 * blocks], refs[1 + 2 * blocks]
    out_ref, packed = refs[-2], refs[-1]
    rows = packed.shape[0]

    @pl.when(pl.program_id(0) == 0)
    def _():
        s, _, _, u = where_am_i(meta_ref)
        width = block_rows
        lead = (s % 2) == 0
        sums = [total_of(r) for r in len_refs]
        starts = [jnp.where(lead, 0, sums[1]), jnp.where(lead, sums[0], 0)]
        if blocks == 4:
            own = sums[0] + sums[1]
            starts += [own + jnp.where(lead, 0, sums[3]), own + jnp.where(lead, sums[2], 0)]
        lane = lax.broadcasted_iota(jnp.int32, (1, width), 1)
        token = lane % tokens
        wanted = lax.broadcasted_iota(jnp.int32, (rows, width), 0)
        picks = []
        for b in range(blocks):
            start = starts[b] + u * span - first
            spot = jnp.full((1, width), -1, jnp.int32)
            for q in range(width // tokens):
                length = len_refs[b][q]
                here = (lane // tokens == q) & (token < length)
                spot = jnp.where(here, start + token, spot)
                start = start + length
            picks.append(jnp.where(spot == wanted, F32(1), F32(0)).astype(BF16))
        pick = jnp.concatenate(picks, axis=1)
        held_rows = jnp.concatenate([r[...] for r in x_refs], axis=0)
        packed[...] = jnp.dot(pick, held_rows, preferred_element_type=F32).astype(BF16)

    out_ref[...] = jnp.dot(packed[...], w_ref[...], preferred_element_type=F32).astype(BF16)


def project(meta, lens, xs, w, first, rows, span, deps=(), tile=512):
    depth, cols = w.shape
    blocks = len(xs)
    block_rows = lens[0].shape[0] * SLOTS
    tokens = SLOTS
    smem = pl.BlockSpec(memory_space=pltpu.SMEM)
    return pl.pallas_call(
        functools.partial(project_kernel, first, blocks, block_rows, tokens, span),
        grid=(cols // tile,),
        in_specs=[smem] * (1 + blocks)
        + [pl.BlockSpec((block_rows, depth), lambda j: (0, 0))] * blocks
        + [pl.BlockSpec((depth, tile), lambda j: (0, j))]
        + [pl.BlockSpec(memory_space=pl.ANY)] * len(deps),
        out_specs=pl.BlockSpec((rows, tile), lambda j: (0, j)),
        out_shape=jax.ShapeDtypeStruct((rows, cols), BF16),
        scratch_shapes=[pltpu.VMEM((rows, depth), BF16)],
        compiler_params=pltpu.CompilerParams(vmem_limit_bytes=VMEM_LIMIT),
        cost_estimate=LIGHT,
    )(meta, *lens, *xs, w, *deps)


def visit(meta_ref, req_ref, slot_ref, flip, held, requests, tokens, act):
    s = meta_ref[0]
    home = s ^ flip
    count = jnp.int32(0)
    for q in range(requests):
        slot = slot_ref[req_ref[home * requests + q]]
        local = lax.rem(slot, held)
        mine = lax.div(slot, held) == s
        row = pl.multiple_of(count * tokens, tokens)

        @pl.when(mine)
        def _():
            act(q, row, local)

        count = count + mine.astype(jnp.int32)


def low_kernel(flips, has_before, held, rank, requests, tokens, *refs):
    meta_ref, req_ref, slot_ref = refs[:3]
    x_refs = refs[3 : 3 + len(flips)]
    down_ref = refs[3 + len(flips)]
    before_ref = refs[4 + len(flips)] if has_before else None
    out_ref, gathered, every = refs[-3:]
    size = out_ref.shape[0] // len(flips)
    lanes = held * rank
    gathered[...] = jnp.zeros(gathered.shape, BF16)
    for i, flip in enumerate(flips):

        def collect(q, row, local, i=i):
            gathered[pl.ds(i * size + row, tokens), :] = x_refs[i][q * tokens : (q + 1) * tokens, :]

        visit(meta_ref, req_ref, slot_ref, flip, held, requests, tokens, collect)
    product = lax.dot_general(
        gathered[...], down_ref[...], (((1,), (1,)), ((), ())), preferred_element_type=F32
    )
    gathered[:, :lanes] = product.astype(BF16)
    every[...] = jnp.zeros(every.shape, BF16)
    group = lax.broadcasted_iota(jnp.int32, (1, lanes), 1) // rank
    for i, flip in enumerate(flips):

        def mask(q, row, local, i=i):
            here = pl.ds(i * size + row, tokens)
            value = gathered[here, :lanes].astype(F32)
            every[here, :] = jnp.where(group == local, value, F32(0)).astype(BF16)

        visit(meta_ref, req_ref, slot_ref, flip, held, requests, tokens, mask)
    source = lax.broadcasted_iota(jnp.int32, (lanes, 2 * rank), 0) % rank
    target = lax.broadcasted_iota(jnp.int32, (lanes, 2 * rank), 1)
    shift = rank if before_ref is not None else 0
    fold = jnp.where(source + shift == target, F32(1), F32(0)).astype(BF16)
    result = jnp.dot(every[...], fold, preferred_element_type=F32)
    if before_ref is not None:
        result = result + before_ref[...].astype(F32)
    out_ref[...] = result.astype(BF16)


def low_rank(meta, req, slot, xs, flips, down_t, before, held, rank, tokens, capacity, deps):
    requests = 2 * capacity
    size = capacity * tokens * len(flips)
    depth = xs[0].shape[1]
    smem = pl.BlockSpec(memory_space=pltpu.SMEM)
    vmem = pl.BlockSpec(memory_space=pltpu.VMEM)
    extra = [] if before is None else [before]
    return pl.pallas_call(
        functools.partial(low_kernel, flips, before is not None, held, rank, requests, tokens),
        in_specs=[smem] * 3 + [vmem] * (len(flips) + 1 + len(extra)) + [pl.BlockSpec(memory_space=pl.ANY)] * len(deps),
        out_specs=vmem,
        out_shape=jax.ShapeDtypeStruct((size, 2 * rank), BF16),
        scratch_shapes=[pltpu.VMEM((size, depth), BF16), pltpu.VMEM((size, held * rank), BF16)],
        compiler_params=pltpu.CompilerParams(vmem_limit_bytes=VMEM_LIMIT),
        cost_estimate=LIGHT,
    )(meta, req, slot, *xs, down_t, *extra, *deps)


def up_kernel(ndeps, held, rank, requests, tokens, meta_ref, req_ref, slot_ref, *refs):
    low_refs, up_ref, out_refs = refs[:4], refs[4], refs[5 + ndeps : 9 + ndeps]
    wide, spread = refs[-2:]
    lanes = held * rank
    half = low_refs[0].shape[0]
    size = half // 2

    @pl.when(pl.program_id(0) == 0)
    def _():
        total = low_refs[0][...].astype(F32)
        for r in low_refs[1:]:
            total = total + r[...].astype(F32)
        total = total.astype(BF16)
        source = lax.broadcasted_iota(jnp.int32, (2 * rank, lanes), 0)
        target = lax.broadcasted_iota(jnp.int32, (2 * rank, lanes), 1) % rank
        for h in range(2):
            tile = jnp.where(source == target + h * rank, F32(1), F32(0)).astype(BF16)
            wide[h * half : (h + 1) * half, :] = jnp.dot(
                total, tile, preferred_element_type=F32
            ).astype(BF16)
        spread[...] = jnp.zeros(spread.shape, BF16)
        group = lax.broadcasted_iota(jnp.int32, (1, lanes), 1) // rank
        for i in range(4):

            def mask(q, row, local, i=i):
                here = pl.ds(i * size + row, tokens)
                value = wide[here, :].astype(F32)
                spread[here, :] = jnp.where(group == local, value, F32(0)).astype(BF16)

            visit(meta_ref, req_ref, slot_ref, i, held, requests, tokens, mask)

    result = jnp.dot(spread[...], up_ref[...], preferred_element_type=F32).astype(BF16)
    for i in range(4):
        out_refs[i][...] = result[i * size : (i + 1) * size, :]


def up_project(meta, req, slot, lows, up_2d, held, rank, tokens, capacity, requests, deps, tile=512):
    cols = up_2d.shape[1]
    size = capacity * tokens
    smem = pl.BlockSpec(memory_space=pltpu.SMEM)
    return pl.pallas_call(
        functools.partial(up_kernel, len(deps), held, rank, requests, tokens),
        grid=(cols // tile,),
        in_specs=[smem] * 3
        + [pl.BlockSpec(lows[0].shape, lambda j: (0, 0))] * 4
        + [pl.BlockSpec((held * rank, tile), lambda j: (0, j))]
        + [pl.BlockSpec(memory_space=pl.ANY)] * len(deps),
        out_specs=[pl.BlockSpec((size, tile), lambda j: (0, j))] * 4,
        out_shape=[jax.ShapeDtypeStruct((size, cols), BF16)] * 4,
        scratch_shapes=[pltpu.VMEM((4 * size, held * rank), BF16)] * 2,
        compiler_params=pltpu.CompilerParams(vmem_limit_bytes=VMEM_LIMIT),
        cost_estimate=LIGHT,
    )(meta, req, slot, *lows, up_2d, *deps)


def extend_kernel(len_ref, x_ref, out_ref):
    rows, depth = x_ref.shape
    extra = out_ref.shape[0] - rows
    out_ref[:rows, :] = x_ref[...]
    lane = lax.broadcasted_iota(jnp.int32, (extra, depth), 1)
    below = jnp.zeros((extra, depth), F32)
    for q in range(len_ref.shape[0]):
        below = jnp.where(lane == q, len_ref[q].astype(F32), below)
    out_ref[rows:, :] = below.astype(BF16)


def extend(lengths, x, extra):
    vmem = pl.BlockSpec(memory_space=pltpu.VMEM)
    return pl.pallas_call(
        extend_kernel,
        in_specs=[pl.BlockSpec(memory_space=pltpu.SMEM), vmem],
        out_specs=vmem,
        out_shape=jax.ShapeDtypeStruct((x.shape[0] + extra, x.shape[1]), BF16),
        compiler_params=pltpu.CompilerParams(vmem_limit_bytes=SMALL_VMEM),
        cost_estimate=LIGHT,
    )(lengths, x)


def keep_kernel(meta_ref, came_ref, own_ref, *refs):
    out_ref, held, sem = refs[-3:]

    @pl.when(meta_ref[0] == meta_ref[1])
    def _():
        for source, target in ((own_ref, held), (held, out_ref)):
            copy = pltpu.make_async_copy(source, target, sem)
            copy.start()
            copy.wait()


def keep(meta, came, own, deps=()):
    anywhere = pl.BlockSpec(memory_space=pl.ANY)
    return pl.pallas_call(
        keep_kernel,
        in_specs=[pl.BlockSpec(memory_space=pltpu.SMEM)] + [anywhere] * (2 + len(deps)),
        out_specs=anywhere,
        out_shape=jax.ShapeDtypeStruct(came.shape, came.dtype),
        scratch_shapes=[pltpu.VMEM(came.shape, came.dtype), pltpu.SemaphoreType.DMA],
        input_output_aliases={1: 0},
        compiler_params=pltpu.CompilerParams(vmem_limit_bytes=SMALL_VMEM),
        cost_estimate=LIGHT,
    )(meta, came, own, *deps)


def merge_kernel(count, streams, has_back, tail, u_ref, *refs):
    out_ref, tail_ref = (refs[-2], refs[-1]) if tail else (refs[-1], None)
    span = refs[0].shape[0]
    for i in range(count):
        at = 0
        for j in range(streams):
            piece = refs[i * streams + j]
            value = piece[...]
            width = piece.shape[1]
            if has_back:
                back = refs[count * streams + i][:, at : at + width]
                value = (value.astype(F32) + back.astype(F32)).astype(BF16)
            out_ref[i * span : (i + 1) * span, at : at + width] = value
            if tail and i == count - 1:
                tail_ref[:, at : at + width] = value
            at += width


def merge(u, pieces, backs, steps_of, tail=False, deps=()):
    count, streams = len(steps_of), len(pieces) // len(steps_of)
    span = pieces[0].shape[0]
    cols = sum(p.shape[1] for p in pieces[:streams])

    def spec_of(low, high, k):
        return pl.BlockSpec((span, cols), lambda i, r: (jnp.clip(k - r[0], low, high) - low, 0))

    specs = [pl.BlockSpec(p.shape, lambda i, r: (0, 0)) for p in pieces]
    specs += [spec_of(low, high, k) for k, (_, low, high) in zip(steps_of, backs)]
    specs += [pl.BlockSpec(memory_space=pl.ANY)] * len(deps)
    sizes = [count * span] + [span] * tail
    return pl.pallas_call(
        functools.partial(merge_kernel, count, streams, bool(backs), tail),
        grid_spec=pltpu.PrefetchScalarGridSpec(
            num_scalar_prefetch=1,
            grid=(1,),
            in_specs=specs,
            out_specs=[pl.BlockSpec((n, cols), lambda i, r: (0, 0)) for n in sizes],
        ),
        out_shape=[jax.ShapeDtypeStruct((n, cols), BF16) for n in sizes],
        compiler_params=pltpu.CompilerParams(vmem_limit_bytes=SMALL_VMEM),
        cost_estimate=LIGHT,
    )(u, *pieces, *[b[0] for b in backs], *deps)


def finish_kernel(n, sizes, first, span, held, requests, tokens, capacity, with_delta, with_acc, *refs):
    meta_ref, req_ref, slot_ref = refs[:3]
    len_refs = refs[3:7]
    at = 7
    value_refs, got_refs = refs[at : at + n], refs[at + n : at + 2 * n]
    at += 2 * n
    delta_refs = refs[at : at + 4] if with_delta else ()
    at += len(delta_refs)
    acc_ref = refs[at] if with_acc else None
    out_ref, picks, dpicks = refs[-3:]
    s, t, _, _ = where_am_i(meta_ref)
    size = capacity * tokens
    keep = (s == t) | (s == (t ^ 2))

    @pl.when(pl.program_id(0) == 0)
    def _():
        flip = 2 * (t // 2)
        key = s ^ flip
        start = jnp.where((t == 0) | (t == 3), 3, 2) * span - first
        for i in range(1, 4):
            start = start + jnp.where(((s ^ i) ^ flip) < key, total_of(len_refs[i]), 0)
        depth = picks.shape[1]
        token = lax.broadcasted_iota(jnp.int32, (tokens, depth), 0)
        base = lax.broadcasted_iota(jnp.int32, (tokens, depth), 1) - token
        wide = dpicks.shape[1]
        dtoken = lax.broadcasted_iota(jnp.int32, (tokens, wide), 0)
        dbase = lax.broadcasted_iota(jnp.int32, (tokens, wide), 1) - dtoken
        counts = [jnp.int32(0)] * 4
        for q in range(requests):
            length = len_refs[0][q]
            here = (base == start) & (token < length)
            picks[q * tokens : (q + 1) * tokens, :] = jnp.where(here, F32(1), F32(0)).astype(BF16)
            start = start + length
            if with_delta:
                owner = lax.div(slot_ref[req_ref[s * requests + q]], held) ^ s
                turn = jnp.int32(0)
                for i in range(4):
                    turn = turn + jnp.where(owner == i, counts[i], 0)
                    counts[i] = counts[i] + jnp.where(owner == i, 1, 0)
                here = (dbase == owner * size + turn * tokens) & (dtoken < length)
                dpicks[q * tokens : (q + 1) * tokens, :] = jnp.where(here, F32(2), F32(0)).astype(BF16)

    def run(group):
        total = None
        for i, (ref, count) in enumerate(zip(group, sizes)):
            offset = sum(sizes[:i])
            part = jnp.dot(picks[:, offset : offset + count], ref[...], preferred_element_type=F32)
            total = part if total is None else total + part
        if with_delta:
            stack = jnp.concatenate([r[...] for r in delta_refs], axis=0)
            total = total + jnp.dot(dpicks[...], stack, preferred_element_type=F32)
        if with_acc:
            total = total + acc_ref[...]
        out_ref[...] = total.astype(out_ref.dtype)

    @pl.when(keep)
    def _():
        run(value_refs)

    @pl.when(jnp.logical_not(keep))
    def _():
        run(got_refs)


def finish(meta, req, slot, lens, values, gots, first, deltas, acc, out_dtype, span, held, tokens, capacity, deps=(), tile=512):
    requests = lens[0].shape[0]
    rows = requests * tokens
    cols = values[0].shape[1]
    sizes = [v.shape[0] for v in values]
    depth = sum(sizes)
    wide = 4 * capacity * tokens
    smem = pl.BlockSpec(memory_space=pltpu.SMEM)
    big = list(values) + list(gots) + list(deltas) + ([] if acc is None else [acc])
    return pl.pallas_call(
        functools.partial(
            finish_kernel,
            len(sizes), sizes, first, span, held, requests, tokens, capacity, bool(deltas), acc is not None,
        ),
        grid=(cols // tile,),
        in_specs=[smem] * 7
        + [pl.BlockSpec((a.shape[0], tile), lambda j: (0, j)) for a in big]
        + [pl.BlockSpec(memory_space=pl.ANY)] * len(deps),
        out_specs=pl.BlockSpec((rows, tile), lambda j: (0, j)),
        out_shape=jax.ShapeDtypeStruct((rows, cols), out_dtype),
        scratch_shapes=[
            pltpu.VMEM((rows, depth), BF16),
            pltpu.VMEM((rows, wide if deltas else 128), BF16),
        ],
        compiler_params=pltpu.CompilerParams(vmem_limit_bytes=SMALL_VMEM),
        cost_estimate=LIGHT,
    )(meta, req, slot, *lens, *big, *deps)


def on_store(value, flip):
    return lax.ppermute(value, "store", [(i, i ^ flip) for i in range(4)])


def plane(s, u):
    return u if s >= 2 else 3 - u


def last_step(s):
    return 3 if s in (0, 3) else 2


def on_mesh(value, pairs):
    return lax.ppermute(value, ("tensor", "store"), [(a * 4 + b, c * 4 + d) for (a, b), (c, d) in pairs])


def square(x, w, down, up, req, slot, lengths):
    requests, tokens, depth = x.shape
    cols = w.shape[1]
    rows = requests * tokens
    live = 3 * rows
    held, _, rank = down.shape
    capacity = requests // 2
    span = SPAN
    steps = live // span
    edge = cols // 2 + 128
    bounds = ((0, edge), (edge, cols))

    s = lax.axis_index("store")
    t = lax.axis_index("tensor")
    meta = jnp.stack([s, t]).astype(jnp.int32)

    x_me = x.reshape(rows, depth)
    x_out = extend(lengths, x_me, tokens)
    x_far = on_store(x_out, 2)
    x_sib = on_store(x_out, 1)

    def lengths_of(array):
        return array[rows, :requests].astype(jnp.int32)

    lens = [lengths, lengths_of(x_sib)]
    xs = [x_me, x_sib]
    down_t = jnp.transpose(down, (0, 2, 1)).reshape(held * rank, depth)
    up_2d = up.reshape(held * rank, cols)

    early = rows // span
    back_pairs = [((plane(b, 3), b), (plane(b, 2), b)) for b in (1, 2)]
    across = [((v, v), (v, v ^ 2)) for v in range(4)]
    beside = [((v, v), (v, v ^ 1)) for v in range(4)] + [((v, v ^ 2), (v, v ^ 3)) for v in range(4)]
    chip = s // 2
    u = jnp.where(chip == 1, t, 3 - t)

    final, carry, parts = {}, [None] * STREAMS, {}

    def chunk_of(source, k, j):
        at = jnp.clip(k - u, 0, steps - 1) * span
        lo, hi = bounds[j]
        return lax.dynamic_slice(source, (at, lo), (span, hi - lo))

    def pairs_of(k):
        return [
            ((plane(b, v), b), (plane(b, v + 1), b))
            for b in range(4)
            for v in range(last_step(b))
            if 0 <= k - v < steps
        ]

    last_pairs = pairs_of(steps + 1)

    def chain_step(k, *deps):
        pairs = pairs_of(k)
        for j in range(STREAMS):
            if k < early:
                value = parts[0][k * span : (k + 1) * span, bounds[j][0] : bounds[j][1]]
            else:
                value = chunk_of(parts[1], k, j)
            if carry[j] is not None:
                came = carry[j]
                if deps and not j:
                    came = after(came, *deps)
                total = value.astype(F32) + came.astype(F32)
                value = total.astype(BF16)
            final[k, j] = value
            carry[j] = on_mesh(value, pairs) if k < steps + 1 else None

    values, gots = [], []

    def merged(lo, hi, tail=False, deps=()):
        ks = range(lo, hi)
        backs = []
        if hi <= steps + 2:
            for k in ks:
                backs.append(next(b for b in back if b[1] <= k - 2 <= b[2]))
        return merge(u_vec, [final[k, j] for k in ks for j in range(STREAMS)], backs, ks, tail, deps)

    def cross(value):
        return on_mesh(value, across), value

    def hand_on(value):
        values.append(value)
        gots.append(on_mesh(value, beside))

    u_vec = u.astype(jnp.int32).reshape(1)
    parts[0] = project(meta, lens[:2], xs[:2], w, 0, early * span, span)
    chain_step(0)
    low = low_rank(
        meta, req, slot, xs[:2], (0, 1), down_t, None, held, rank, tokens, capacity, (parts[0],)
    )
    chain_step(1)
    x_far = after(x_far, final[1, 0], final[1, 1], low)
    x_fsib = on_store(x_far, 1)
    xs = [x_me, x_sib, x_far, x_fsib]
    lens = lens + [lengths_of(x_far), lengths_of(x_fsib)]
    parts[1] = project(meta, lens, xs, w, 0, live, 0)
    chain_step(2)
    low = low_rank(
        meta, req, slot, xs[2:], (2, 3), down_t, low, held, rank, tokens, capacity, (final[2, 0], final[2, 1])
    )
    lows = [low] + [lax.ppermute(low, "tensor", [(i, i ^ f) for i in range(4)]) for f in (1, 2, 3)]
    chain_step(3, low)
    delta = up_project(
        meta, req, slot, lows, up_2d, held, rank, tokens, capacity, requests, (final[3, 0], final[3, 1])
    )
    deltas = [delta[0]] + [on_store(delta[i], i) for i in (1, 2, 3)]
    chain_step(4, delta[0])
    cut = steps - 2

    def send_back(low, high, *deps):
        rows_of = after(parts[1][low * span : (high + 1) * span], *deps)
        return on_mesh(rows_of, back_pairs), low, high

    back = [send_back(0, cut - 1, final[4, 0], final[4, 1])]
    chain_step(5, deltas[1])
    back.append(send_back(cut, steps - 1, final[5, 0], final[5, 1]))
    chain_step(6, deltas[2])
    (two,) = merged(4, 6)
    chain_step(7, two, deltas[3])
    two = keep(meta, *cross(two))
    three, last = merged(6, 8, True)
    came = on_mesh(last, last_pairs)
    (one,) = merged(2, 4, deps=(last,))
    three = cross(three)
    hand_on(one)
    (four,) = merge(u_vec, [came], [(parts[1], 0, steps - 1)], [steps + 2], deps=(two,))
    hand_on(two)
    partial = finish(
        meta, req, slot, lens, values[:1], gots[:1], 2 * span, deltas, None, F32, span, held, tokens, capacity,
        (four,),
    )
    hand_on(keep(meta, *three, (partial,)))
    hand_on(keep(meta, *cross(four)))
    out = finish(
        meta, req, slot, lens, values[1:], gots[1:], 4 * span, (), partial, BF16, span, held, tokens, capacity
    )
    return out.reshape(requests, tokens, cols)


def solution(mesh):
    in_specs = (
        P(("groups", "store"), None, "tensor"),
        P("tensor", "store"),
        P("store", "tensor", None),
        P("store", None, "tensor"),
        P("groups"),
        P("groups"),
        P(("groups", "store")),
    )
    out_specs = P(("groups", "store"), None, "tensor")
    four = mesh.shape["store"] == 4 and mesh.shape["tensor"] == 4
    body = square if four else general
    return jax.shard_map(body, mesh=mesh, in_specs=in_specs, out_specs=out_specs, check_vma=False)
```

```python
import functools
import jax
import jax.numpy as jnp
from jax import lax
from jax.experimental import pallas as pl
from jax.experimental.pallas import tpu as pltpu
from jax.sharding import PartitionSpec as P

VMEM_LIMIT = 52 * 1024 * 1024
SMALL_VMEM = 32 * 1024 * 1024
STREAMS = 2
SPAN = 128
SLOTS = 16
BF16 = jnp.bfloat16
F32 = jnp.float32
LIGHT = pl.CostEstimate(flops=0, bytes_accessed=0, transcendentals=0)


def general(
    attention_input,
    base_projection_weight,
    stored_down_maps,
    stored_up_maps,
    request_adapter_index,
    adapter_store_slot,
    lengths,
):
    requests, seq_len, width_in = attention_input.shape
    owner_grouping = stored_down_maps.shape[0]
    stores = lax.axis_size("store")
    my_index = lax.axis_index("store")
    capacity = (2 * requests + stores - 1) // stores
    partial_value = jnp.einsum(
        "qtk,kd->qtd",
        attention_input,
        lax.all_gather(base_projection_weight, "store", axis=1, tiled=True),
        preferred_element_type=jnp.float32,
    )
    base_out = lax.psum_scatter(
        partial_value.astype(jnp.bfloat16), "tensor", scatter_dimension=2, tiled=True
    ).astype(jnp.float32)
    slot_all = adapter_store_slot[request_adapter_index]
    owner_all = (slot_all // owner_grouping).reshape(stores, requests)
    local_all = (slot_all % owner_grouping).reshape(stores, requests)
    positions = jnp.arange(requests, dtype=jnp.int32)
    earlier = positions[None, :] < positions[:, None]
    same_owner = owner_all[:, :, None] == owner_all[:, None, :]
    rank_all = jnp.sum(same_owner & earlier[None], axis=2)
    owner_mine = lax.dynamic_index_in_dim(owner_all, my_index, 0, keepdims=False)
    rank_mine = lax.dynamic_index_in_dim(rank_all, my_index, 0, keepdims=False)
    owner_range = jnp.arange(stores, dtype=jnp.int32)
    slot_range = jnp.arange(capacity, dtype=jnp.int32)
    local_range = jnp.arange(owner_grouping, dtype=jnp.int32)
    pick_table = (
        (owner_mine[:, None, None] == owner_range[None, :, None])
        & (rank_mine[:, None, None] == slot_range[None, None, :])
    ).astype(jnp.bfloat16)
    selection_matrix = jnp.sum(
        (
            (owner_all == my_index)[:, :, None, None]
            & (rank_all[:, :, None, None] == slot_range[None, None, :, None])
            & (local_all[:, :, None, None] == local_range[None, None, None, :])
        ).astype(jnp.float32),
        axis=1,
    ).astype(jnp.bfloat16)
    outgoing = jnp.einsum(
        "qoc,qtk->octk", pick_table, attention_input, preferred_element_type=jnp.float32
    ).astype(jnp.bfloat16)
    arrived = lax.all_to_all(outgoing, "store", split_axis=0, concat_axis=0, tiled=True)
    down_sel = jnp.einsum(
        "pmb,bwf->pmwf", selection_matrix, stored_down_maps, preferred_element_type=jnp.float32
    ).astype(jnp.bfloat16)
    up_sel = jnp.einsum(
        "ehw,wkx->ehkx", selection_matrix, stored_up_maps, preferred_element_type=jnp.float32
    ).astype(jnp.bfloat16)
    low_part = jnp.einsum("octk,ockr->octr", arrived, down_sel, preferred_element_type=jnp.float32)
    low_full = lax.psum(low_part.astype(jnp.bfloat16), "tensor")
    delta_rows = jnp.einsum(
        "octr,ocrd->octd", low_full, up_sel, preferred_element_type=jnp.float32
    ).astype(jnp.bfloat16)
    returned = lax.all_to_all(delta_rows, "store", split_axis=0, concat_axis=0, tiled=True)
    my_delta = jnp.einsum("qoc,octd->qtd", pick_table, returned, preferred_element_type=jnp.float32)
    token_slots = jnp.arange(seq_len, dtype=jnp.int32)
    valid_mask = (token_slots[None, :] < lengths[:, None]).astype(jnp.float32)
    total = base_out + 2.0 * my_delta
    return (total * valid_mask[:, :, None]).astype(jnp.bfloat16)


def where_am_i(meta_ref):
    s, t = meta_ref[0], meta_ref[1]
    chip = s // 2
    return s, t, chip, jnp.where(chip == 1, t, 3 - t)


def total_of(ref):
    total = ref[0]
    for q in range(1, ref.shape[0]):
        total = total + ref[q]
    return total


def tie_kernel(*refs):
    pass


def after(value, *deps):
    anywhere = pl.BlockSpec(memory_space=pl.ANY)
    return pl.pallas_call(
        tie_kernel,
        in_specs=[anywhere] * (1 + len(deps)),
        out_specs=anywhere,
        out_shape=jax.ShapeDtypeStruct(value.shape, value.dtype),
        input_output_aliases={0: 0},
        cost_estimate=LIGHT,
    )(value, *deps)


def project_kernel(first, blocks, block_rows, tokens, *refs):
    meta_ref, len_refs = refs[0], refs[1 : 1 + blocks]
    x_refs, w_ref = refs[1 + blocks : 1 + 2 * blocks], refs[1 + 2 * blocks]
    out_ref, packed = refs[-2], refs[-1]
    rows, width = packed.shape[0], block_rows

    @pl.when(pl.program_id(0) == 0)
    def _():
        s = meta_ref[0]
        lead = (s % 2) == 0
        sums = [total_of(r) for r in len_refs]
        starts = [jnp.where(lead, 0, sums[1]), jnp.where(lead, sums[0], 0)]
        if blocks == 4:
            own = sums[0] + sums[1]
            starts += [own + jnp.where(lead, 0, sums[3]), own + jnp.where(lead, sums[2], 0)]
        lane = lax.broadcasted_iota(jnp.int32, (1, width), 1)
        token = lane % tokens
        wanted = lax.broadcasted_iota(jnp.int32, (rows, width), 0)
        picks = []
        for b in range(blocks):
            start = starts[b] - first
            spot = jnp.full((1, width), -1, jnp.int32)
            for q in range(width // tokens):
                length = len_refs[b][q]
                here = (lane // tokens == q) & (token < length)
                spot = jnp.where(here, start + token, spot)
                start = start + length
            picks.append(jnp.where(spot == wanted, F32(1), F32(0)).astype(BF16))
        pick = jnp.concatenate(picks, axis=1)
        held_rows = jnp.concatenate([r[...] for r in x_refs], axis=0)
        packed[...] = jnp.dot(pick, held_rows, preferred_element_type=F32).astype(BF16)

    out_ref[...] = jnp.dot(packed[...], w_ref[...], preferred_element_type=F32).astype(BF16)


def project(meta, lens, xs, w, first, rows, total, place, buffer=None, deps=(), tile=512):
    depth, cols = w.shape
    blocks = len(xs)
    tokens = SLOTS
    width = lens[0].shape[0] * tokens
    smem = pl.BlockSpec(memory_space=pltpu.SMEM)
    extra = ([] if buffer is None else [buffer]) + list(deps)
    return pl.pallas_call(
        functools.partial(project_kernel, first, blocks, width, tokens),
        grid=(cols // tile,),
        in_specs=[smem] * (1 + blocks)
        + [pl.BlockSpec((width, depth), lambda j: (0, 0))] * blocks
        + [pl.BlockSpec((depth, tile), lambda j: (0, j))]
        + [pl.BlockSpec(memory_space=pl.ANY)] * len(extra),
        out_specs=pl.BlockSpec((rows, tile), lambda j: (place, j)),
        out_shape=jax.ShapeDtypeStruct((total, cols), BF16),
        scratch_shapes=[pltpu.VMEM((rows, depth), BF16)],
        input_output_aliases={} if buffer is None else {2 + 2 * blocks: 0},
        compiler_params=pltpu.CompilerParams(vmem_limit_bytes=VMEM_LIMIT),
        cost_estimate=LIGHT,
    )(meta, *lens, *xs, w, *extra)


def visit(meta_ref, req_ref, slot_ref, flip, held, requests, tokens, act):
    s = meta_ref[0]
    home = s ^ flip
    count = jnp.int32(0)
    for q in range(requests):
        slot = slot_ref[req_ref[home * requests + q]]
        local = lax.rem(slot, held)
        mine = lax.div(slot, held) == s
        row = pl.multiple_of(count * tokens, tokens)

        @pl.when(mine)
        def _():
            act(q, row, local)

        count = count + mine.astype(jnp.int32)


def low_kernel(flips, has_before, held, rank, requests, tokens, *refs):
    meta_ref, req_ref, slot_ref = refs[:3]
    x_refs = refs[3 : 3 + len(flips)]
    down_ref = refs[3 + len(flips)]
    before_ref = refs[4 + len(flips)] if has_before else None
    out_ref, gathered, every = refs[-3:]
    size = out_ref.shape[0] // len(flips)
    lanes = held * rank
    gathered[...] = jnp.zeros(gathered.shape, BF16)
    for i, flip in enumerate(flips):

        def collect(q, row, local, i=i):
            gathered[pl.ds(i * size + row, tokens), :] = x_refs[i][q * tokens : (q + 1) * tokens, :]

        visit(meta_ref, req_ref, slot_ref, flip, held, requests, tokens, collect)
    product = lax.dot_general(
        gathered[...], down_ref[...], (((1,), (1,)), ((), ())), preferred_element_type=F32
    )
    gathered[:, :lanes] = product.astype(BF16)
    every[...] = jnp.zeros(every.shape, BF16)
    group = lax.broadcasted_iota(jnp.int32, (1, lanes), 1) // rank
    for i, flip in enumerate(flips):

        def mask(q, row, local, i=i):
            here = pl.ds(i * size + row, tokens)
            value = gathered[here, :lanes].astype(F32)
            every[here, :] = jnp.where(group == local, value, F32(0)).astype(BF16)

        visit(meta_ref, req_ref, slot_ref, flip, held, requests, tokens, mask)
    source = lax.broadcasted_iota(jnp.int32, (lanes, 2 * rank), 0) % rank
    target = lax.broadcasted_iota(jnp.int32, (lanes, 2 * rank), 1)
    shift = rank if before_ref is not None else 0
    fold = jnp.where(source + shift == target, F32(1), F32(0)).astype(BF16)
    result = jnp.dot(every[...], fold, preferred_element_type=F32)
    if before_ref is not None:
        result = result + before_ref[...].astype(F32)
    out_ref[...] = result.astype(BF16)


def low_rank(meta, req, slot, xs, flips, down_t, before, held, rank, tokens, capacity, deps):
    requests = 2 * capacity
    size = capacity * tokens * len(flips)
    depth = xs[0].shape[1]
    smem = pl.BlockSpec(memory_space=pltpu.SMEM)
    vmem = pl.BlockSpec(memory_space=pltpu.VMEM)
    extra = [] if before is None else [before]
    return pl.pallas_call(
        functools.partial(low_kernel, flips, before is not None, held, rank, requests, tokens),
        in_specs=[smem] * 3 + [vmem] * (len(flips) + 1 + len(extra)) + [pl.BlockSpec(memory_space=pl.ANY)] * len(deps),
        out_specs=vmem,
        out_shape=jax.ShapeDtypeStruct((size, 2 * rank), BF16),
        scratch_shapes=[pltpu.VMEM((size, depth), BF16), pltpu.VMEM((size, held * rank), BF16)],
        compiler_params=pltpu.CompilerParams(vmem_limit_bytes=VMEM_LIMIT),
        cost_estimate=LIGHT,
    )(meta, req, slot, *xs, down_t, *extra, *deps)


def up_kernel(ndeps, held, rank, requests, tokens, meta_ref, req_ref, slot_ref, *refs):
    low_refs, up_ref, out_refs = refs[:4], refs[4], refs[5 + ndeps : 9 + ndeps]
    wide, spread = refs[-2:]
    lanes = held * rank
    half = low_refs[0].shape[0]
    size = half // 2

    @pl.when(pl.program_id(0) == 0)
    def _():
        total = low_refs[0][...].astype(F32)
        for r in low_refs[1:]:
            total = total + r[...].astype(F32)
        total = total.astype(BF16)
        source = lax.broadcasted_iota(jnp.int32, (2 * rank, lanes), 0)
        target = lax.broadcasted_iota(jnp.int32, (2 * rank, lanes), 1) % rank
        for h in range(2):
            tile = jnp.where(source == target + h * rank, F32(1), F32(0)).astype(BF16)
            wide[h * half : (h + 1) * half, :] = jnp.dot(
                total, tile, preferred_element_type=F32
            ).astype(BF16)
        spread[...] = jnp.zeros(spread.shape, BF16)
        group = lax.broadcasted_iota(jnp.int32, (1, lanes), 1) // rank
        for i in range(4):

            def mask(q, row, local, i=i):
                here = pl.ds(i * size + row, tokens)
                value = wide[here, :].astype(F32)
                spread[here, :] = jnp.where(group == local, value, F32(0)).astype(BF16)

            visit(meta_ref, req_ref, slot_ref, i, held, requests, tokens, mask)

    result = jnp.dot(spread[...], up_ref[...], preferred_element_type=F32).astype(BF16)
    for i in range(4):
        out_refs[i][...] = result[i * size : (i + 1) * size, :]


def up_project(meta, req, slot, lows, up_2d, held, rank, tokens, capacity, requests, deps, tile=512):
    cols = up_2d.shape[1]
    size = capacity * tokens
    smem = pl.BlockSpec(memory_space=pltpu.SMEM)
    return pl.pallas_call(
        functools.partial(up_kernel, len(deps), held, rank, requests, tokens),
        grid=(cols // tile,),
        in_specs=[smem] * 3
        + [pl.BlockSpec(lows[0].shape, lambda j: (0, 0))] * 4
        + [pl.BlockSpec((held * rank, tile), lambda j: (0, j))]
        + [pl.BlockSpec(memory_space=pl.ANY)] * len(deps),
        out_specs=[pl.BlockSpec((size, tile), lambda j: (0, j))] * 4,
        out_shape=[jax.ShapeDtypeStruct((size, cols), BF16)] * 4,
        scratch_shapes=[pltpu.VMEM((4 * size, held * rank), BF16)] * 2,
        compiler_params=pltpu.CompilerParams(vmem_limit_bytes=VMEM_LIMIT),
        cost_estimate=LIGHT,
    )(meta, req, slot, *lows, up_2d, *deps)


def extend_kernel(len_ref, x_ref, out_ref):
    rows, depth = x_ref.shape
    extra = out_ref.shape[0] - rows
    out_ref[:rows, :] = x_ref[...]
    lane = lax.broadcasted_iota(jnp.int32, (extra, depth), 1)
    below = jnp.zeros((extra, depth), F32)
    for q in range(len_ref.shape[0]):
        below = jnp.where(lane == q, len_ref[q].astype(F32), below)
    out_ref[rows:, :] = below.astype(BF16)


def extend(lengths, x, extra):
    vmem = pl.BlockSpec(memory_space=pltpu.VMEM)
    return pl.pallas_call(
        extend_kernel,
        in_specs=[pl.BlockSpec(memory_space=pltpu.SMEM), vmem],
        out_specs=vmem,
        out_shape=jax.ShapeDtypeStruct((x.shape[0] + extra, x.shape[1]), BF16),
        compiler_params=pltpu.CompilerParams(vmem_limit_bytes=SMALL_VMEM),
        cost_estimate=LIGHT,
    )(lengths, x)


def keep_kernel(meta_ref, came_ref, own_ref, *refs):
    out_ref, held, sem = refs[-3:]

    @pl.when(meta_ref[0] == meta_ref[1])
    def _():
        for source, target in ((own_ref, held), (held, out_ref)):
            copy = pltpu.make_async_copy(source, target, sem)
            copy.start()
            copy.wait()


def keep(meta, came, own, deps=()):
    anywhere = pl.BlockSpec(memory_space=pl.ANY)
    return pl.pallas_call(
        keep_kernel,
        in_specs=[pl.BlockSpec(memory_space=pltpu.SMEM)] + [anywhere] * (2 + len(deps)),
        out_specs=anywhere,
        out_shape=jax.ShapeDtypeStruct(came.shape, came.dtype),
        scratch_shapes=[pltpu.VMEM(came.shape, came.dtype), pltpu.SemaphoreType.DMA],
        input_output_aliases={1: 0},
        compiler_params=pltpu.CompilerParams(vmem_limit_bytes=SMALL_VMEM),
        cost_estimate=LIGHT,
    )(meta, came, own, *deps)


def merge_kernel(count, streams, has_back, tail, u_ref, *refs):
    out_ref, tail_ref = (refs[-2], refs[-1]) if tail else (refs[-1], None)
    span = refs[0].shape[0]
    for i in range(count):
        at = 0
        for j in range(streams):
            piece = refs[i * streams + j]
            value = piece[...]
            width = piece.shape[1]
            if has_back:
                back = refs[count * streams + i][:, at : at + width]
                value = (value.astype(F32) + back.astype(F32)).astype(BF16)
            out_ref[i * span : (i + 1) * span, at : at + width] = value
            if tail and i == count - 1:
                tail_ref[:, at : at + width] = value
            at += width


def merge(u, pieces, backs, steps_of, tail=False, deps=()):
    count, streams = len(steps_of), len(pieces) // len(steps_of)
    span = pieces[0].shape[0]
    cols = sum(p.shape[1] for p in pieces[:streams])

    def spec_of(low, high, k):
        return pl.BlockSpec((span, cols), lambda i, r: (jnp.clip(k - r[0], low, high) - low, 0))

    specs = [pl.BlockSpec(p.shape, lambda i, r: (0, 0)) for p in pieces]
    specs += [spec_of(low, high, k) for k, (_, low, high) in zip(steps_of, backs)]
    specs += [pl.BlockSpec(memory_space=pl.ANY)] * len(deps)
    sizes = [count * span] + [span] * tail
    return pl.pallas_call(
        functools.partial(merge_kernel, count, streams, bool(backs), tail),
        grid_spec=pltpu.PrefetchScalarGridSpec(
            num_scalar_prefetch=1,
            grid=(1,),
            in_specs=specs,
            out_specs=[pl.BlockSpec((n, cols), lambda i, r: (0, 0)) for n in sizes],
        ),
        out_shape=[jax.ShapeDtypeStruct((n, cols), BF16) for n in sizes],
        compiler_params=pltpu.CompilerParams(vmem_limit_bytes=SMALL_VMEM),
        cost_estimate=LIGHT,
    )(u, *pieces, *[b[0] for b in backs], *deps)


def finish_kernel(n, sizes, first, span, held, requests, tokens, capacity, with_delta, with_acc, *refs):
    meta_ref, req_ref, slot_ref = refs[:3]
    len_refs = refs[3:7]
    at = 7
    value_refs, got_refs = refs[at : at + n], refs[at + n : at + 2 * n]
    at += 2 * n
    delta_refs = refs[at : at + 4] if with_delta else ()
    at += len(delta_refs)
    acc_ref = refs[at] if with_acc else None
    out_ref, picks, dpicks = refs[-3:]
    s, t, _, _ = where_am_i(meta_ref)
    size = capacity * tokens
    keep = (s == t) | (s == (t ^ 2))

    @pl.when(pl.program_id(0) == 0)
    def _():
        flip = 2 * (t // 2)
        key = s ^ flip
        start = jnp.where((t == 0) | (t == 3), 3, 2) * span - first
        for i in range(1, 4):
            start = start + jnp.where(((s ^ i) ^ flip) < key, total_of(len_refs[i]), 0)
        depth = picks.shape[1]
        token = lax.broadcasted_iota(jnp.int32, (tokens, depth), 0)
        base = lax.broadcasted_iota(jnp.int32, (tokens, depth), 1) - token
        wide = dpicks.shape[1]
        dtoken = lax.broadcasted_iota(jnp.int32, (tokens, wide), 0)
        dbase = lax.broadcasted_iota(jnp.int32, (tokens, wide), 1) - dtoken
        counts = [jnp.int32(0)] * 4
        for q in range(requests):
            length = len_refs[0][q]
            here = (base == start) & (token < length)
            picks[q * tokens : (q + 1) * tokens, :] = jnp.where(here, F32(1), F32(0)).astype(BF16)
            start = start + length
            if with_delta:
                owner = lax.div(slot_ref[req_ref[s * requests + q]], held) ^ s
                turn = jnp.int32(0)
                for i in range(4):
                    turn = turn + jnp.where(owner == i, counts[i], 0)
                    counts[i] = counts[i] + jnp.where(owner == i, 1, 0)
                here = (dbase == owner * size + turn * tokens) & (dtoken < length)
                dpicks[q * tokens : (q + 1) * tokens, :] = jnp.where(here, F32(2), F32(0)).astype(BF16)

    def run(group):
        total = None
        for i, (ref, count) in enumerate(zip(group, sizes)):
            offset = sum(sizes[:i])
            part = jnp.dot(picks[:, offset : offset + count], ref[...], preferred_element_type=F32)
            total = part if total is None else total + part
        if with_delta:
            stack = jnp.concatenate([r[...] for r in delta_refs], axis=0)
            total = total + jnp.dot(dpicks[...], stack, preferred_element_type=F32)
        if with_acc:
            total = total + acc_ref[...]
        out_ref[...] = total.astype(out_ref.dtype)

    @pl.when(keep)
    def _():
        run(value_refs)

    @pl.when(jnp.logical_not(keep))
    def _():
        run(got_refs)


def finish(meta, req, slot, lens, values, gots, first, deltas, acc, out_dtype, span, held, tokens, capacity, deps=(), tile=512):
    requests = lens[0].shape[0]
    rows = requests * tokens
    cols = values[0].shape[1]
    sizes = [v.shape[0] for v in values]
    depth = sum(sizes)
    wide = 4 * capacity * tokens
    smem = pl.BlockSpec(memory_space=pltpu.SMEM)
    big = list(values) + list(gots) + list(deltas) + ([] if acc is None else [acc])
    return pl.pallas_call(
        functools.partial(
            finish_kernel,
            len(sizes), sizes, first, span, held, requests, tokens, capacity, bool(deltas), acc is not None,
        ),
        grid=(cols // tile,),
        in_specs=[smem] * 7
        + [pl.BlockSpec((a.shape[0], tile), lambda j: (0, j)) for a in big]
        + [pl.BlockSpec(memory_space=pl.ANY)] * len(deps),
        out_specs=pl.BlockSpec((rows, tile), lambda j: (0, j)),
        out_shape=jax.ShapeDtypeStruct((rows, cols), out_dtype),
        scratch_shapes=[
            pltpu.VMEM((rows, depth), BF16),
            pltpu.VMEM((rows, wide if deltas else 128), BF16),
        ],
        compiler_params=pltpu.CompilerParams(vmem_limit_bytes=SMALL_VMEM),
        cost_estimate=LIGHT,
    )(meta, req, slot, *lens, *big, *deps)


def on_store(value, flip):
    return lax.ppermute(value, "store", [(i, i ^ flip) for i in range(4)])


def plane(s, u):
    return u if s >= 2 else 3 - u


def last_step(s):
    return 3 if s in (0, 3) else 2


def on_mesh(value, pairs):
    return lax.ppermute(value, ("tensor", "store"), [(a * 4 + b, c * 4 + d) for (a, b), (c, d) in pairs])


def square(x, w, down, up, req, slot, lengths):
    requests, tokens, depth = x.shape
    cols = w.shape[1]
    rows = requests * tokens
    live = 3 * rows
    held, _, rank = down.shape
    capacity = requests // 2
    span = SPAN
    steps = live // span
    edge = cols // 2 + 128
    bounds = ((0, edge), (edge, cols))

    s = lax.axis_index("store")
    t = lax.axis_index("tensor")
    meta = jnp.stack([s, t]).astype(jnp.int32)

    x_me = x.reshape(rows, depth)
    x_out = extend(lengths, x_me, tokens)
    x_far = on_store(x_out, 2)
    x_sib = on_store(x_out, 1)

    def lengths_of(array):
        return array[rows, :requests].astype(jnp.int32)

    lens = [lengths, lengths_of(x_sib)]
    xs = [x_me, x_sib]
    down_t = jnp.transpose(down, (0, 2, 1)).reshape(held * rank, depth)
    up_2d = up.reshape(held * rank, cols)

    early = rows // span
    back_pairs = [((plane(b, 3), b), (plane(b, 2), b)) for b in (1, 2)]
    across = [((v, v), (v, v ^ 2)) for v in range(4)]
    beside = [((v, v), (v, v ^ 1)) for v in range(4)] + [((v, v ^ 2), (v, v ^ 3)) for v in range(4)]
    chip = s // 2
    u = jnp.where(chip == 1, t, 3 - t)

    final, carry, parts = {}, [None] * STREAMS, {}

    def chunk_of(source, k, j):
        c = jnp.clip(k - u, 0, steps - 1)
        at = jnp.where(c < early, c + steps - early, c - early) * span
        lo, hi = bounds[j]
        return lax.dynamic_slice(source, (at, lo), (span, hi - lo))

    def first_chunk(c, j):
        at = (c + steps - early) * span
        return parts[0][at : at + span, bounds[j][0] : bounds[j][1]]

    def pairs_of(k):
        return [
            ((plane(b, v), b), (plane(b, v + 1), b))
            for b in range(4)
            for v in range(last_step(b))
            if 0 <= k - v < steps
        ]

    last_pairs = pairs_of(steps + 1)

    def chain_step(k, *deps, both=False):
        pairs = pairs_of(k)
        for j in range(STREAMS):
            if k < early:
                value = first_chunk(0, j)
                for c in range(1, k + 1):
                    value = jnp.where(k - u >= c, first_chunk(c, j), value)
            else:
                value = chunk_of(parts[1], k, j)
            if carry[j] is not None:
                came = carry[j]
                if deps and (both or not j):
                    came = after(came, *deps)
                total = value.astype(F32) + came.astype(F32)
                value = total.astype(BF16)
            final[k, j] = value
            carry[j] = on_mesh(value, pairs) if k < steps + 1 else None

    values, gots = [], []

    def merged(lo, hi, tail=False, deps=()):
        ks = range(lo, hi)
        backs = []
        if hi <= steps + 2:
            for k in ks:
                backs.append(next(b for b in back if b[1] <= k - 2 <= b[2]))
        return merge(u_vec, [final[k, j] for k in ks for j in range(STREAMS)], backs, ks, tail, deps)

    def cross(value):
        return on_mesh(value, across), value

    def hand_on(value):
        values.append(value)
        gots.append(on_mesh(value, beside))

    u_vec = u.astype(jnp.int32).reshape(1)
    parts[0] = project(meta, lens[:2], xs[:2], w, 0, rows, live, live // rows - 1)
    chain_step(0)
    low = low_rank(
        meta, req, slot, xs[:2], (0, 1), down_t, None, held, rank, tokens, capacity, (parts[0],)
    )
    chain_step(1)
    x_far = after(x_far, final[1, 0], final[1, 1], low)
    x_fsib = on_store(x_far, 1)
    xs = [x_me, x_sib, x_far, x_fsib]
    lens = lens + [lengths_of(x_far), lengths_of(x_fsib)]
    parts[1] = project(
        meta, lens, xs, w, rows, live - rows, live, 0, parts[0], (final[1, 0], final[1, 1])
    )
    chain_step(2)
    low = low_rank(
        meta, req, slot, xs[2:], (2, 3), down_t, low, held, rank, tokens, capacity, (final[2, 0], final[2, 1])
    )
    lows = [low] + [lax.ppermute(low, "tensor", [(i, i ^ f) for i in range(4)]) for f in (3, 1, 2)]
    chain_step(3, low)
    delta = up_project(
        meta, req, slot, lows, up_2d, held, rank, tokens, capacity, requests, (final[3, 0], final[3, 1])
    )
    deltas = [delta[0]] + [on_store(delta[i], i) for i in (1, 2, 3)]
    chain_step(4, delta[0])

    def send_back(low, high, *deps):
        at = (low - early if low >= early else low + steps - early) * span
        rows_of = after(parts[1][at : at + (high + 1 - low) * span], *deps)
        return on_mesh(rows_of, back_pairs), low, high

    back = [send_back(early, steps - 1, final[4, 0], final[4, 1])]
    chain_step(5, deltas[1])
    back.append(send_back(0, early - 1, final[5, 0], final[5, 1]))
    chain_step(6, deltas[2])
    (two,) = merged(4, 6)
    (one,) = merged(2, 4, deps=(two,))
    hand_on(one)
    chain_step(7, two, deltas[3], one, both=True)
    two = keep(meta, *cross(two))
    three, last = merged(6, 8, True)
    came = on_mesh(last, last_pairs)
    three = cross(three)
    (four,) = merge(u_vec, [came], [(parts[1], early, steps - 1)], [steps + 2], deps=(two,))
    hand_on(two)
    partial = finish(
        meta, req, slot, lens, values[:1], gots[:1], 2 * span, deltas, None, F32, span, held, tokens, capacity,
        (four,),
    )
    hand_on(keep(meta, *three, (partial,)))
    hand_on(keep(meta, *cross(four)))
    out = finish(
        meta, req, slot, lens, values[1:], gots[1:], 4 * span, (), partial, BF16, span, held, tokens, capacity
    )
    return out.reshape(requests, tokens, cols)


def solution(mesh):
    in_specs = (
        P(("groups", "store"), None, "tensor"),
        P("tensor", "store"),
        P("store", "tensor", None),
        P("store", None, "tensor"),
        P("groups"),
        P("groups"),
        P(("groups", "store")),
    )
    out_specs = P(("groups", "store"), None, "tensor")
    four = mesh.shape["store"] == 4 and mesh.shape["tensor"] == 4
    body = square if four else general
    return jax.shard_map(body, mesh=mesh, in_specs=in_specs, out_specs=out_specs, check_vma=False)
```

```python
import functools
import jax
import jax.numpy as jnp
from jax import lax
from jax.experimental import pallas as pl
from jax.experimental.pallas import tpu as pltpu
from jax.sharding import PartitionSpec as P

VMEM_LIMIT = 52 * 1024 * 1024
SMALL_VMEM = 32 * 1024 * 1024
STREAMS = 2
SPAN = 128
SLOTS = 16
BF16 = jnp.bfloat16
F32 = jnp.float32
LIGHT = pl.CostEstimate(flops=0, bytes_accessed=0, transcendentals=0)


def general(
    attention_input,
    base_projection_weight,
    stored_down_maps,
    stored_up_maps,
    request_adapter_index,
    adapter_store_slot,
    lengths,
):
    requests, seq_len, width_in = attention_input.shape
    owner_grouping = stored_down_maps.shape[0]
    stores = lax.axis_size("store")
    my_index = lax.axis_index("store")
    capacity = (2 * requests + stores - 1) // stores
    partial_value = jnp.einsum(
        "qtk,kd->qtd",
        attention_input,
        lax.all_gather(base_projection_weight, "store", axis=1, tiled=True),
        preferred_element_type=jnp.float32,
    )
    base_out = lax.psum_scatter(
        partial_value.astype(jnp.bfloat16), "tensor", scatter_dimension=2, tiled=True
    ).astype(jnp.float32)
    slot_all = adapter_store_slot[request_adapter_index]
    owner_all = (slot_all // owner_grouping).reshape(stores, requests)
    local_all = (slot_all % owner_grouping).reshape(stores, requests)
    positions = jnp.arange(requests, dtype=jnp.int32)
    earlier = positions[None, :] < positions[:, None]
    same_owner = owner_all[:, :, None] == owner_all[:, None, :]
    rank_all = jnp.sum(same_owner & earlier[None], axis=2)
    owner_mine = lax.dynamic_index_in_dim(owner_all, my_index, 0, keepdims=False)
    rank_mine = lax.dynamic_index_in_dim(rank_all, my_index, 0, keepdims=False)
    owner_range = jnp.arange(stores, dtype=jnp.int32)
    slot_range = jnp.arange(capacity, dtype=jnp.int32)
    local_range = jnp.arange(owner_grouping, dtype=jnp.int32)
    pick_table = (
        (owner_mine[:, None, None] == owner_range[None, :, None])
        & (rank_mine[:, None, None] == slot_range[None, None, :])
    ).astype(jnp.bfloat16)
    selection_matrix = jnp.sum(
        (
            (owner_all == my_index)[:, :, None, None]
            & (rank_all[:, :, None, None] == slot_range[None, None, :, None])
            & (local_all[:, :, None, None] == local_range[None, None, None, :])
        ).astype(jnp.float32),
        axis=1,
    ).astype(jnp.bfloat16)
    outgoing = jnp.einsum(
        "qoc,qtk->octk", pick_table, attention_input, preferred_element_type=jnp.float32
    ).astype(jnp.bfloat16)
    arrived = lax.all_to_all(outgoing, "store", split_axis=0, concat_axis=0, tiled=True)
    down_sel = jnp.einsum(
        "pmb,bwf->pmwf", selection_matrix, stored_down_maps, preferred_element_type=jnp.float32
    ).astype(jnp.bfloat16)
    up_sel = jnp.einsum(
        "ehw,wkx->ehkx", selection_matrix, stored_up_maps, preferred_element_type=jnp.float32
    ).astype(jnp.bfloat16)
    low_part = jnp.einsum("octk,ockr->octr", arrived, down_sel, preferred_element_type=jnp.float32)
    low_full = lax.psum(low_part.astype(jnp.bfloat16), "tensor")
    delta_rows = jnp.einsum(
        "octr,ocrd->octd", low_full, up_sel, preferred_element_type=jnp.float32
    ).astype(jnp.bfloat16)
    returned = lax.all_to_all(delta_rows, "store", split_axis=0, concat_axis=0, tiled=True)
    my_delta = jnp.einsum("qoc,octd->qtd", pick_table, returned, preferred_element_type=jnp.float32)
    token_slots = jnp.arange(seq_len, dtype=jnp.int32)
    valid_mask = (token_slots[None, :] < lengths[:, None]).astype(jnp.float32)
    total = base_out + 2.0 * my_delta
    return (total * valid_mask[:, :, None]).astype(jnp.bfloat16)


def where_am_i(meta_ref):
    s, t = meta_ref[0], meta_ref[1]
    chip = s // 2
    return s, t, chip, jnp.where(chip == 1, t, 3 - t)


def total_of(ref):
    total = ref[0]
    for q in range(1, ref.shape[0]):
        total = total + ref[q]
    return total


def tie_kernel(*refs):
    pass


def after(value, *deps):
    anywhere = pl.BlockSpec(memory_space=pl.ANY)
    return pl.pallas_call(
        tie_kernel,
        in_specs=[anywhere] * (1 + len(deps)),
        out_specs=anywhere,
        out_shape=jax.ShapeDtypeStruct(value.shape, value.dtype),
        input_output_aliases={0: 0},
        cost_estimate=LIGHT,
    )(value, *deps)


def project_kernel(first, blocks, block_rows, tokens, *refs):
    meta_ref, len_refs = refs[0], refs[1 : 1 + blocks]
    x_refs, w_ref = refs[1 + blocks : 1 + 2 * blocks], refs[1 + 2 * blocks]
    out_ref, packed = refs[-2], refs[-1]
    rows, width = packed.shape[0], block_rows

    @pl.when(pl.program_id(0) == 0)
    def _():
        s = meta_ref[0]
        lead = (s % 2) == 0
        sums = [total_of(r) for r in len_refs]
        starts = [jnp.where(lead, 0, sums[1]), jnp.where(lead, sums[0], 0)]
        if blocks == 4:
            own = sums[0] + sums[1]
            starts += [own + jnp.where(lead, 0, sums[3]), own + jnp.where(lead, sums[2], 0)]
        lane = lax.broadcasted_iota(jnp.int32, (1, width), 1)
        token = lane % tokens
        wanted = lax.broadcasted_iota(jnp.int32, (rows, width), 0)
        picks = []
        for b in range(blocks):
            start = starts[b] - first
            spot = jnp.full((1, width), -1, jnp.int32)
            for q in range(width // tokens):
                length = len_refs[b][q]
                here = (lane // tokens == q) & (token < length)
                spot = jnp.where(here, start + token, spot)
                start = start + length
            picks.append(jnp.where(spot == wanted, F32(1), F32(0)).astype(BF16))
        pick = jnp.concatenate(picks, axis=1)
        held_rows = jnp.concatenate([r[...] for r in x_refs], axis=0)
        packed[...] = jnp.dot(pick, held_rows, preferred_element_type=F32).astype(BF16)

    out_ref[...] = jnp.dot(packed[...], w_ref[...], preferred_element_type=F32).astype(BF16)


def project(meta, lens, xs, w, first, rows, total, place, buffer=None, deps=(), tile=1024):
    depth, cols = w.shape
    blocks = len(xs)
    tokens = SLOTS
    width = lens[0].shape[0] * tokens
    smem = pl.BlockSpec(memory_space=pltpu.SMEM)
    extra = ([] if buffer is None else [buffer]) + list(deps)
    return pl.pallas_call(
        functools.partial(project_kernel, first, blocks, width, tokens),
        grid=(cols // tile,),
        in_specs=[smem] * (1 + blocks)
        + [pl.BlockSpec((width, depth), lambda j: (0, 0))] * blocks
        + [pl.BlockSpec((depth, tile), lambda j: (0, j))]
        + [pl.BlockSpec(memory_space=pl.ANY)] * len(extra),
        out_specs=pl.BlockSpec((rows, tile), lambda j: (place, j)),
        out_shape=jax.ShapeDtypeStruct((total, cols), BF16),
        scratch_shapes=[pltpu.VMEM((rows, depth), BF16)],
        input_output_aliases={} if buffer is None else {2 + 2 * blocks: 0},
        compiler_params=pltpu.CompilerParams(vmem_limit_bytes=VMEM_LIMIT),
        cost_estimate=LIGHT,
    )(meta, *lens, *xs, w, *extra)


def visit(meta_ref, req_ref, slot_ref, flip, held, requests, tokens, act):
    s = meta_ref[0]
    home = s ^ flip
    count = jnp.int32(0)
    for q in range(requests):
        slot = slot_ref[req_ref[home * requests + q]]
        local = lax.rem(slot, held)
        mine = lax.div(slot, held) == s
        row = pl.multiple_of(count * tokens, tokens)

        @pl.when(mine)
        def _():
            act(q, row, local)

        count = count + mine.astype(jnp.int32)


def low_kernel(flips, has_before, held, rank, requests, tokens, *refs):
    meta_ref, req_ref, slot_ref = refs[:3]
    x_refs = refs[3 : 3 + len(flips)]
    down_ref = refs[3 + len(flips)]
    before_ref = refs[4 + len(flips)] if has_before else None
    out_ref, gathered, every = refs[-3:]
    size = out_ref.shape[0] // len(flips)
    lanes = held * rank
    gathered[...] = jnp.zeros(gathered.shape, BF16)
    for i, flip in enumerate(flips):

        def collect(q, row, local, i=i):
            gathered[pl.ds(i * size + row, tokens), :] = x_refs[i][q * tokens : (q + 1) * tokens, :]

        visit(meta_ref, req_ref, slot_ref, flip, held, requests, tokens, collect)
    product = lax.dot_general(
        gathered[...], down_ref[...], (((1,), (1,)), ((), ())), preferred_element_type=F32
    )
    gathered[:, :lanes] = product.astype(BF16)
    every[...] = jnp.zeros(every.shape, BF16)
    group = lax.broadcasted_iota(jnp.int32, (1, lanes), 1) // rank
    for i, flip in enumerate(flips):

        def mask(q, row, local, i=i):
            here = pl.ds(i * size + row, tokens)
            value = gathered[here, :lanes].astype(F32)
            every[here, :] = jnp.where(group == local, value, F32(0)).astype(BF16)

        visit(meta_ref, req_ref, slot_ref, flip, held, requests, tokens, mask)
    source = lax.broadcasted_iota(jnp.int32, (lanes, 2 * rank), 0) % rank
    target = lax.broadcasted_iota(jnp.int32, (lanes, 2 * rank), 1)
    shift = rank if before_ref is not None else 0
    fold = jnp.where(source + shift == target, F32(1), F32(0)).astype(BF16)
    result = jnp.dot(every[...], fold, preferred_element_type=F32)
    if before_ref is not None:
        result = result + before_ref[...].astype(F32)
    out_ref[...] = result.astype(BF16)


def low_rank(meta, req, slot, xs, flips, down_t, before, held, rank, tokens, capacity, deps):
    requests = 2 * capacity
    size = capacity * tokens * len(flips)
    depth = xs[0].shape[1]
    smem = pl.BlockSpec(memory_space=pltpu.SMEM)
    vmem = pl.BlockSpec(memory_space=pltpu.VMEM)
    extra = [] if before is None else [before]
    return pl.pallas_call(
        functools.partial(low_kernel, flips, before is not None, held, rank, requests, tokens),
        in_specs=[smem] * 3 + [vmem] * (len(flips) + 1 + len(extra)) + [pl.BlockSpec(memory_space=pl.ANY)] * len(deps),
        out_specs=vmem,
        out_shape=jax.ShapeDtypeStruct((size, 2 * rank), BF16),
        scratch_shapes=[pltpu.VMEM((size, depth), BF16), pltpu.VMEM((size, held * rank), BF16)],
        compiler_params=pltpu.CompilerParams(vmem_limit_bytes=VMEM_LIMIT),
        cost_estimate=LIGHT,
    )(meta, req, slot, *xs, down_t, *extra, *deps)


def up_kernel(ndeps, held, rank, requests, tokens, meta_ref, req_ref, slot_ref, *refs):
    low_refs, up_ref, out_refs = refs[:4], refs[4], refs[5 + ndeps : 9 + ndeps]
    wide, spread = refs[-2:]
    lanes = held * rank
    half = low_refs[0].shape[0]
    size = half // 2

    @pl.when(pl.program_id(0) == 0)
    def _():
        total = low_refs[0][...].astype(F32)
        for r in low_refs[1:]:
            total = total + r[...].astype(F32)
        total = total.astype(BF16)
        source = lax.broadcasted_iota(jnp.int32, (2 * rank, lanes), 0)
        target = lax.broadcasted_iota(jnp.int32, (2 * rank, lanes), 1) % rank
        for h in range(2):
            tile = jnp.where(source == target + h * rank, F32(1), F32(0)).astype(BF16)
            wide[h * half : (h + 1) * half, :] = jnp.dot(
                total, tile, preferred_element_type=F32
            ).astype(BF16)
        spread[...] = jnp.zeros(spread.shape, BF16)
        group = lax.broadcasted_iota(jnp.int32, (1, lanes), 1) // rank
        for i in range(4):

            def mask(q, row, local, i=i):
                here = pl.ds(i * size + row, tokens)
                value = wide[here, :].astype(F32)
                spread[here, :] = jnp.where(group == local, value, F32(0)).astype(BF16)

            visit(meta_ref, req_ref, slot_ref, i, held, requests, tokens, mask)

    result = jnp.dot(spread[...], up_ref[...], preferred_element_type=F32).astype(BF16)
    for i in range(4):
        out_refs[i][...] = result[i * size : (i + 1) * size, :]


def up_project(meta, req, slot, lows, up_2d, held, rank, tokens, capacity, requests, deps, tile=1024):
    cols = up_2d.shape[1]
    size = capacity * tokens
    smem = pl.BlockSpec(memory_space=pltpu.SMEM)
    return pl.pallas_call(
        functools.partial(up_kernel, len(deps), held, rank, requests, tokens),
        grid=(cols // tile,),
        in_specs=[smem] * 3
        + [pl.BlockSpec(lows[0].shape, lambda j: (0, 0))] * 4
        + [pl.BlockSpec((held * rank, tile), lambda j: (0, j))]
        + [pl.BlockSpec(memory_space=pl.ANY)] * len(deps),
        out_specs=[pl.BlockSpec((size, tile), lambda j: (0, j))] * 4,
        out_shape=[jax.ShapeDtypeStruct((size, cols), BF16)] * 4,
        scratch_shapes=[pltpu.VMEM((4 * size, held * rank), BF16)] * 2,
        compiler_params=pltpu.CompilerParams(vmem_limit_bytes=VMEM_LIMIT),
        cost_estimate=LIGHT,
    )(meta, req, slot, *lows, up_2d, *deps)


def extend_kernel(len_ref, x_ref, out_ref):
    rows, depth = x_ref.shape
    extra = out_ref.shape[0] - rows
    out_ref[:rows, :] = x_ref[...]
    lane = lax.broadcasted_iota(jnp.int32, (extra, depth), 1)
    below = jnp.zeros((extra, depth), F32)
    for q in range(len_ref.shape[0]):
        below = jnp.where(lane == q, len_ref[q].astype(F32), below)
    out_ref[rows:, :] = below.astype(BF16)


def extend(lengths, x, extra):
    vmem = pl.BlockSpec(memory_space=pltpu.VMEM)
    return pl.pallas_call(
        extend_kernel,
        in_specs=[pl.BlockSpec(memory_space=pltpu.SMEM), vmem],
        out_specs=vmem,
        out_shape=jax.ShapeDtypeStruct((x.shape[0] + extra, x.shape[1]), BF16),
        compiler_params=pltpu.CompilerParams(vmem_limit_bytes=SMALL_VMEM),
        cost_estimate=LIGHT,
    )(lengths, x)


def keep_kernel(meta_ref, came_ref, own_ref, *refs):
    out_ref, held, sem = refs[-3:]

    @pl.when(meta_ref[0] == meta_ref[1])
    def _():
        for source, target in ((own_ref, held), (held, out_ref)):
            copy = pltpu.make_async_copy(source, target, sem)
            copy.start()
            copy.wait()


def keep(meta, came, own, deps=()):
    anywhere = pl.BlockSpec(memory_space=pl.ANY)
    return pl.pallas_call(
        keep_kernel,
        in_specs=[pl.BlockSpec(memory_space=pltpu.SMEM)] + [anywhere] * (2 + len(deps)),
        out_specs=anywhere,
        out_shape=jax.ShapeDtypeStruct(came.shape, came.dtype),
        scratch_shapes=[pltpu.VMEM(came.shape, came.dtype), pltpu.SemaphoreType.DMA],
        input_output_aliases={1: 0},
        compiler_params=pltpu.CompilerParams(vmem_limit_bytes=SMALL_VMEM),
        cost_estimate=LIGHT,
    )(meta, came, own, *deps)


def merge_kernel(count, streams, has_back, tail, u_ref, *refs):
    out_ref, tail_ref = (refs[-2], refs[-1]) if tail else (refs[-1], None)
    span = refs[0].shape[0]
    for i in range(count):
        at = 0
        for j in range(streams):
            piece = refs[i * streams + j]
            value = piece[...]
            width = piece.shape[1]
            if has_back:
                back = refs[count * streams + i][:, at : at + width]
                value = (value.astype(F32) + back.astype(F32)).astype(BF16)
            out_ref[i * span : (i + 1) * span, at : at + width] = value
            if tail and i == count - 1:
                tail_ref[:, at : at + width] = value
            at += width


def merge(u, pieces, backs, steps_of, tail=False, deps=()):
    count, streams = len(steps_of), len(pieces) // len(steps_of)
    span = pieces[0].shape[0]
    cols = sum(p.shape[1] for p in pieces[:streams])

    def spec_of(low, high, k):
        return pl.BlockSpec((span, cols), lambda i, r: (jnp.clip(k - r[0], low, high) - low, 0))

    specs = [pl.BlockSpec(p.shape, lambda i, r: (0, 0)) for p in pieces]
    specs += [spec_of(low, high, k) for k, (_, low, high) in zip(steps_of, backs)]
    specs += [pl.BlockSpec(memory_space=pl.ANY)] * len(deps)
    sizes = [count * span] + [span] * tail
    return pl.pallas_call(
        functools.partial(merge_kernel, count, streams, bool(backs), tail),
        grid_spec=pltpu.PrefetchScalarGridSpec(
            num_scalar_prefetch=1,
            grid=(1,),
            in_specs=specs,
            out_specs=[pl.BlockSpec((n, cols), lambda i, r: (0, 0)) for n in sizes],
        ),
        out_shape=[jax.ShapeDtypeStruct((n, cols), BF16) for n in sizes],
        compiler_params=pltpu.CompilerParams(vmem_limit_bytes=SMALL_VMEM),
        cost_estimate=LIGHT,
    )(u, *pieces, *[b[0] for b in backs], *deps)


def finish_kernel(n, sizes, first, span, held, requests, tokens, capacity, with_delta, with_acc, *refs):
    meta_ref, req_ref, slot_ref = refs[:3]
    len_refs = refs[3:7]
    at = 7
    value_refs, got_refs = refs[at : at + n], refs[at + n : at + 2 * n]
    at += 2 * n
    delta_refs = refs[at : at + 4] if with_delta else ()
    at += len(delta_refs)
    acc_ref = refs[at] if with_acc else None
    out_ref, picks, dpicks = refs[-3:]
    s, t, _, _ = where_am_i(meta_ref)
    size = capacity * tokens
    keep = (s == t) | (s == (t ^ 2))

    @pl.when(pl.program_id(0) == 0)
    def _():
        flip = 2 * (t // 2)
        key = s ^ flip
        start = jnp.where((t == 0) | (t == 3), 3, 2) * span - first
        for i in range(1, 4):
            start = start + jnp.where(((s ^ i) ^ flip) < key, total_of(len_refs[i]), 0)
        depth = picks.shape[1]
        token = lax.broadcasted_iota(jnp.int32, (tokens, depth), 0)
        base = lax.broadcasted_iota(jnp.int32, (tokens, depth), 1) - token
        wide = dpicks.shape[1]
        dtoken = lax.broadcasted_iota(jnp.int32, (tokens, wide), 0)
        dbase = lax.broadcasted_iota(jnp.int32, (tokens, wide), 1) - dtoken
        counts = [jnp.int32(0)] * 4
        for q in range(requests):
            length = len_refs[0][q]
            here = (base == start) & (token < length)
            picks[q * tokens : (q + 1) * tokens, :] = jnp.where(here, F32(1), F32(0)).astype(BF16)
            start = start + length
            if with_delta:
                owner = lax.div(slot_ref[req_ref[s * requests + q]], held) ^ s
                turn = jnp.int32(0)
                for i in range(4):
                    turn = turn + jnp.where(owner == i, counts[i], 0)
                    counts[i] = counts[i] + jnp.where(owner == i, 1, 0)
                here = (dbase == owner * size + turn * tokens) & (dtoken < length)
                dpicks[q * tokens : (q + 1) * tokens, :] = jnp.where(here, F32(2), F32(0)).astype(BF16)

    def run(group):
        total = None
        for i, (ref, count) in enumerate(zip(group, sizes)):
            offset = sum(sizes[:i])
            part = jnp.dot(picks[:, offset : offset + count], ref[...], preferred_element_type=F32)
            total = part if total is None else total + part
        if with_delta:
            stack = jnp.concatenate([r[...] for r in delta_refs], axis=0)
            total = total + jnp.dot(dpicks[...], stack, preferred_element_type=F32)
        if with_acc:
            total = total + acc_ref[...]
        out_ref[...] = total.astype(out_ref.dtype)

    @pl.when(keep)
    def _():
        run(value_refs)

    @pl.when(jnp.logical_not(keep))
    def _():
        run(got_refs)


def finish(meta, req, slot, lens, values, gots, first, deltas, acc, out_dtype, span, held, tokens, capacity, deps=(), tile=1024):
    requests = lens[0].shape[0]
    rows = requests * tokens
    cols = values[0].shape[1]
    sizes = [v.shape[0] for v in values]
    depth = sum(sizes)
    wide = 4 * capacity * tokens
    smem = pl.BlockSpec(memory_space=pltpu.SMEM)
    big = list(values) + list(gots) + list(deltas) + ([] if acc is None else [acc])
    return pl.pallas_call(
        functools.partial(
            finish_kernel,
            len(sizes), sizes, first, span, held, requests, tokens, capacity, bool(deltas), acc is not None,
        ),
        grid=(cols // tile,),
        in_specs=[smem] * 7
        + [pl.BlockSpec((a.shape[0], tile), lambda j: (0, j)) for a in big]
        + [pl.BlockSpec(memory_space=pl.ANY)] * len(deps),
        out_specs=pl.BlockSpec((rows, tile), lambda j: (0, j)),
        out_shape=jax.ShapeDtypeStruct((rows, cols), out_dtype),
        scratch_shapes=[
            pltpu.VMEM((rows, depth), BF16),
            pltpu.VMEM((rows, wide if deltas else 128), BF16),
        ],
        compiler_params=pltpu.CompilerParams(vmem_limit_bytes=SMALL_VMEM),
        cost_estimate=LIGHT,
    )(meta, req, slot, *lens, *big, *deps)


def on_store(value, flip):
    return lax.ppermute(value, "store", [(i, i ^ flip) for i in range(4)])


def plane(s, u):
    return u if s >= 2 else 3 - u


def last_step(s):
    return 3 if s in (0, 3) else 2


def on_mesh(value, pairs):
    return lax.ppermute(value, ("tensor", "store"), [(a * 4 + b, c * 4 + d) for (a, b), (c, d) in pairs])


def square(x, w, down, up, req, slot, lengths):
    requests, tokens, depth = x.shape
    cols = w.shape[1]
    rows = requests * tokens
    live = 3 * rows
    held, _, rank = down.shape
    capacity = requests // 2
    span = SPAN
    steps = live // span
    edge = cols // 2 + 128
    bounds = ((0, edge), (edge, cols))

    s = lax.axis_index("store")
    t = lax.axis_index("tensor")
    meta = jnp.stack([s, t]).astype(jnp.int32)

    x_me = x.reshape(rows, depth)
    x_out = extend(lengths, x_me, tokens)
    x_far = on_store(x_out, 2)
    x_sib = on_store(x_out, 1)

    def lengths_of(array):
        return array[rows, :requests].astype(jnp.int32)

    lens = [lengths, lengths_of(x_sib)]
    xs = [x_me, x_sib]
    down_t = jnp.transpose(down, (0, 2, 1)).reshape(held * rank, depth)
    up_2d = up.reshape(held * rank, cols)

    early = rows // span
    back_pairs = [((plane(b, 3), b), (plane(b, 2), b)) for b in (1, 2)]
    across = [((v, v), (v, v ^ 2)) for v in range(4)]
    beside = [((v, v), (v, v ^ 1)) for v in range(4)] + [((v, v ^ 2), (v, v ^ 3)) for v in range(4)]
    chip = s // 2
    u = jnp.where(chip == 1, t, 3 - t)

    final, carry, parts = {}, [None] * STREAMS, {}

    def chunk_of(source, k, j):
        c = jnp.clip(k - u, 0, steps - 1)
        at = jnp.where(c < early, c + steps - early, c - early) * span
        lo, hi = bounds[j]
        return lax.dynamic_slice(source, (at, lo), (span, hi - lo))

    def first_chunk(c, j):
        at = (c + steps - early) * span
        return parts[0][at : at + span, bounds[j][0] : bounds[j][1]]

    def pairs_of(k):
        return [
            ((plane(b, v), b), (plane(b, v + 1), b))
            for b in range(4)
            for v in range(last_step(b))
            if 0 <= k - v < steps
        ]

    last_pairs = pairs_of(steps + 1)

    def chain_step(k, *deps, both=False):
        pairs = pairs_of(k)
        for j in range(STREAMS):
            if k < early:
                value = first_chunk(0, j)
                for c in range(1, k + 1):
                    value = jnp.where(k - u >= c, first_chunk(c, j), value)
            else:
                value = chunk_of(parts[1], k, j)
            if carry[j] is not None:
                came = carry[j]
                if deps and (both or not j):
                    came = after(came, *deps)
                total = value.astype(F32) + came.astype(F32)
                value = total.astype(BF16)
            final[k, j] = value
            carry[j] = on_mesh(value, pairs) if k < steps + 1 else None

    values, gots = [], []

    def merged(lo, hi, tail=False, deps=()):
        ks = range(lo, hi)
        backs = []
        if hi <= steps + 2:
            for k in ks:
                backs.append(next(b for b in back if b[1] <= k - 2 <= b[2]))
        return merge(u_vec, [final[k, j] for k in ks for j in range(STREAMS)], backs, ks, tail, deps)

    def cross(value):
        return on_mesh(value, across), value

    def hand_on(value):
        values.append(value)
        gots.append(on_mesh(value, beside))

    u_vec = u.astype(jnp.int32).reshape(1)
    parts[0] = project(meta, lens[:2], xs[:2], w, 0, rows, live, live // rows - 1)
    chain_step(0)
    low = low_rank(
        meta, req, slot, xs[:2], (0, 1), down_t, None, held, rank, tokens, capacity, (parts[0],)
    )
    chain_step(1)
    x_far = after(x_far, final[1, 0], final[1, 1], low)
    x_fsib = on_store(x_far, 1)
    xs = [x_me, x_sib, x_far, x_fsib]
    lens = lens + [lengths_of(x_far), lengths_of(x_fsib)]
    parts[1] = project(
        meta, lens, xs, w, rows, live - rows, live, 0, parts[0], (final[1, 0], final[1, 1])
    )
    chain_step(2)
    low = low_rank(
        meta, req, slot, xs[2:], (2, 3), down_t, low, held, rank, tokens, capacity, (final[2, 0], final[2, 1])
    )
    lows = [low] + [lax.ppermute(low, "tensor", [(i, i ^ f) for i in range(4)]) for f in (3, 1, 2)]
    chain_step(3, low)
    delta = up_project(
        meta, req, slot, lows, up_2d, held, rank, tokens, capacity, requests, (final[3, 0], final[3, 1])
    )
    deltas = [delta[0]] + [on_store(delta[i], i) for i in (1, 2, 3)]
    chain_step(4, delta[0])

    def send_back(low, high, *deps):
        at = (low - early if low >= early else low + steps - early) * span
        rows_of = after(parts[1][at : at + (high + 1 - low) * span], *deps)
        return on_mesh(rows_of, back_pairs), low, high

    back = [send_back(early, steps - 1, final[4, 0], final[4, 1])]
    chain_step(5, deltas[1])
    back.append(send_back(0, early - 1, final[5, 0], final[5, 1]))
    chain_step(6, deltas[2])
    (two,) = merged(4, 6)
    (one,) = merged(2, 4, deps=(two,))
    hand_on(one)
    chain_step(7, two, deltas[3], one, both=True)
    two = keep(meta, *cross(two))
    three, last = merged(6, 8, True)
    came = on_mesh(last, last_pairs)
    three = cross(three)
    (four,) = merge(u_vec, [came], [(parts[1], early, steps - 1)], [steps + 2], deps=(two,))
    hand_on(two)
    partial = finish(
        meta, req, slot, lens, values[:1], gots[:1], 2 * span, deltas, None, F32, span, held, tokens, capacity,
        (four,),
    )
    hand_on(keep(meta, *three, (partial,)))
    hand_on(keep(meta, *cross(four)))
    out = finish(
        meta, req, slot, lens, values[1:], gots[1:], 4 * span, (), partial, BF16, span, held, tokens, capacity
    )
    return out.reshape(requests, tokens, cols)


def solution(mesh):
    in_specs = (
        P(("groups", "store"), None, "tensor"),
        P("tensor", "store"),
        P("store", "tensor", None),
        P("store", None, "tensor"),
        P("groups"),
        P("groups"),
        P(("groups", "store")),
    )
    out_specs = P(("groups", "store"), None, "tensor")
    four = mesh.shape["store"] == 4 and mesh.shape["tensor"] == 4
    body = square if four else general
    return jax.shard_map(body, mesh=mesh, in_specs=in_specs, out_specs=out_specs, check_vma=False)
```

```python
import functools
import jax
import jax.numpy as jnp
from jax import lax
from jax.experimental import pallas as pl
from jax.experimental.pallas import tpu as pltpu
from jax.sharding import PartitionSpec as P

VMEM_LIMIT = 52 * 1024 * 1024
SMALL_VMEM = 32 * 1024 * 1024
STREAMS = 2
SPAN = 128
SLOTS = 16
BF16 = jnp.bfloat16
F32 = jnp.float32
LIGHT = pl.CostEstimate(flops=0, bytes_accessed=0, transcendentals=0)


def general(
    attention_input,
    base_projection_weight,
    stored_down_maps,
    stored_up_maps,
    request_adapter_index,
    adapter_store_slot,
    lengths,
):
    requests, seq_len, width_in = attention_input.shape
    owner_grouping = stored_down_maps.shape[0]
    stores = lax.axis_size("store")
    my_index = lax.axis_index("store")
    capacity = (2 * requests + stores - 1) // stores
    partial_value = jnp.einsum(
        "qtk,kd->qtd",
        attention_input,
        lax.all_gather(base_projection_weight, "store", axis=1, tiled=True),
        preferred_element_type=jnp.float32,
    )
    base_out = lax.psum_scatter(
        partial_value.astype(jnp.bfloat16), "tensor", scatter_dimension=2, tiled=True
    ).astype(jnp.float32)
    slot_all = adapter_store_slot[request_adapter_index]
    owner_all = (slot_all // owner_grouping).reshape(stores, requests)
    local_all = (slot_all % owner_grouping).reshape(stores, requests)
    positions = jnp.arange(requests, dtype=jnp.int32)
    earlier = positions[None, :] < positions[:, None]
    same_owner = owner_all[:, :, None] == owner_all[:, None, :]
    rank_all = jnp.sum(same_owner & earlier[None], axis=2)
    owner_mine = lax.dynamic_index_in_dim(owner_all, my_index, 0, keepdims=False)
    rank_mine = lax.dynamic_index_in_dim(rank_all, my_index, 0, keepdims=False)
    owner_range = jnp.arange(stores, dtype=jnp.int32)
    slot_range = jnp.arange(capacity, dtype=jnp.int32)
    local_range = jnp.arange(owner_grouping, dtype=jnp.int32)
    pick_table = (
        (owner_mine[:, None, None] == owner_range[None, :, None])
        & (rank_mine[:, None, None] == slot_range[None, None, :])
    ).astype(jnp.bfloat16)
    selection_matrix = jnp.sum(
        (
            (owner_all == my_index)[:, :, None, None]
            & (rank_all[:, :, None, None] == slot_range[None, None, :, None])
            & (local_all[:, :, None, None] == local_range[None, None, None, :])
        ).astype(jnp.float32),
        axis=1,
    ).astype(jnp.bfloat16)
    outgoing = jnp.einsum(
        "qoc,qtk->octk", pick_table, attention_input, preferred_element_type=jnp.float32
    ).astype(jnp.bfloat16)
    arrived = lax.all_to_all(outgoing, "store", split_axis=0, concat_axis=0, tiled=True)
    down_sel = jnp.einsum(
        "pmb,bwf->pmwf", selection_matrix, stored_down_maps, preferred_element_type=jnp.float32
    ).astype(jnp.bfloat16)
    up_sel = jnp.einsum(
        "ehw,wkx->ehkx", selection_matrix, stored_up_maps, preferred_element_type=jnp.float32
    ).astype(jnp.bfloat16)
    low_part = jnp.einsum("octk,ockr->octr", arrived, down_sel, preferred_element_type=jnp.float32)
    low_full = lax.psum(low_part.astype(jnp.bfloat16), "tensor")
    delta_rows = jnp.einsum(
        "octr,ocrd->octd", low_full, up_sel, preferred_element_type=jnp.float32
    ).astype(jnp.bfloat16)
    returned = lax.all_to_all(delta_rows, "store", split_axis=0, concat_axis=0, tiled=True)
    my_delta = jnp.einsum("qoc,octd->qtd", pick_table, returned, preferred_element_type=jnp.float32)
    token_slots = jnp.arange(seq_len, dtype=jnp.int32)
    valid_mask = (token_slots[None, :] < lengths[:, None]).astype(jnp.float32)
    total = base_out + 2.0 * my_delta
    return (total * valid_mask[:, :, None]).astype(jnp.bfloat16)


def where_am_i(meta_ref):
    s, t = meta_ref[0], meta_ref[1]
    chip = s // 2
    return s, t, chip, jnp.where(chip == 1, t, 3 - t)


def total_of(ref):
    total = ref[0]
    for q in range(1, ref.shape[0]):
        total = total + ref[q]
    return total


def tie_kernel(*refs):
    pass


def after(value, *deps):
    anywhere = pl.BlockSpec(memory_space=pl.ANY)
    return pl.pallas_call(
        tie_kernel,
        in_specs=[anywhere] * (1 + len(deps)),
        out_specs=anywhere,
        out_shape=jax.ShapeDtypeStruct(value.shape, value.dtype),
        input_output_aliases={0: 0},
        cost_estimate=LIGHT,
    )(value, *deps)


def project_kernel(first, blocks, block_rows, tokens, *refs):
    meta_ref, len_refs = refs[0], refs[1 : 1 + blocks]
    x_refs, w_ref = refs[1 + blocks : 1 + 2 * blocks], refs[1 + 2 * blocks]
    out_ref, packed = refs[-2], refs[-1]
    rows, width = packed.shape[0], block_rows

    @pl.when(pl.program_id(0) == 0)
    def _():
        s = meta_ref[0]
        lead = (s % 2) == 0
        sums = [total_of(r) for r in len_refs]
        starts = [jnp.where(lead, 0, sums[1]), jnp.where(lead, sums[0], 0)]
        if blocks == 4:
            own = sums[0] + sums[1]
            starts += [own + jnp.where(lead, 0, sums[3]), own + jnp.where(lead, sums[2], 0)]
        lane = lax.broadcasted_iota(jnp.int32, (1, width), 1)
        token = lane % tokens
        wanted = lax.broadcasted_iota(jnp.int32, (rows, width), 0)
        picks = []
        for b in range(blocks):
            start = starts[b] - first
            spot = jnp.full((1, width), -1, jnp.int32)
            for q in range(width // tokens):
                length = len_refs[b][q]
                here = (lane // tokens == q) & (token < length)
                spot = jnp.where(here, start + token, spot)
                start = start + length
            picks.append(jnp.where(spot == wanted, F32(1), F32(0)).astype(BF16))
        pick = jnp.concatenate(picks, axis=1)
        held_rows = jnp.concatenate([r[...] for r in x_refs], axis=0)
        packed[...] = jnp.dot(pick, held_rows, preferred_element_type=F32).astype(BF16)

    out_ref[...] = jnp.dot(packed[...], w_ref[...], preferred_element_type=F32).astype(BF16)


def project(meta, lens, xs, w, first, rows, total, place, buffer=None, deps=(), tile=1024):
    depth, cols = w.shape
    blocks = len(xs)
    tokens = SLOTS
    width = lens[0].shape[0] * tokens
    smem = pl.BlockSpec(memory_space=pltpu.SMEM)
    extra = ([] if buffer is None else [buffer]) + list(deps)
    return pl.pallas_call(
        functools.partial(project_kernel, first, blocks, width, tokens),
        grid=(cols // tile,),
        in_specs=[smem] * (1 + blocks)
        + [pl.BlockSpec((width, depth), lambda j: (0, 0))] * blocks
        + [pl.BlockSpec((depth, tile), lambda j: (0, j))]
        + [pl.BlockSpec(memory_space=pl.ANY)] * len(extra),
        out_specs=pl.BlockSpec((rows, tile), lambda j: (place, j)),
        out_shape=jax.ShapeDtypeStruct((total, cols), BF16),
        scratch_shapes=[pltpu.VMEM((rows, depth), BF16)],
        input_output_aliases={} if buffer is None else {2 + 2 * blocks: 0},
        compiler_params=pltpu.CompilerParams(vmem_limit_bytes=VMEM_LIMIT),
        cost_estimate=LIGHT,
    )(meta, *lens, *xs, w, *extra)


def visit(meta_ref, req_ref, slot_ref, flip, held, requests, tokens, act):
    s = meta_ref[0]
    home = s ^ flip
    count = jnp.int32(0)
    for q in range(requests):
        slot = slot_ref[req_ref[home * requests + q]]
        local = lax.rem(slot, held)
        mine = lax.div(slot, held) == s
        row = pl.multiple_of(count * tokens, tokens)

        @pl.when(mine)
        def _():
            act(q, row, local)

        count = count + mine.astype(jnp.int32)


def low_kernel(flips, has_before, held, rank, requests, tokens, *refs):
    meta_ref, req_ref, slot_ref = refs[:3]
    x_refs = refs[3 : 3 + len(flips)]
    down_ref = refs[3 + len(flips)]
    before_ref = refs[4 + len(flips)] if has_before else None
    out_ref, gathered, every = refs[-3:]
    size = out_ref.shape[0] // len(flips)
    lanes = held * rank
    gathered[...] = jnp.zeros(gathered.shape, BF16)
    for i, flip in enumerate(flips):

        def collect(q, row, local, i=i):
            gathered[pl.ds(i * size + row, tokens), :] = x_refs[i][q * tokens : (q + 1) * tokens, :]

        visit(meta_ref, req_ref, slot_ref, flip, held, requests, tokens, collect)
    product = lax.dot_general(
        gathered[...], down_ref[...], (((1,), (1,)), ((), ())), preferred_element_type=F32
    )
    gathered[:, :lanes] = product.astype(BF16)
    every[...] = jnp.zeros(every.shape, BF16)
    group = lax.broadcasted_iota(jnp.int32, (1, lanes), 1) // rank
    for i, flip in enumerate(flips):

        def mask(q, row, local, i=i):
            here = pl.ds(i * size + row, tokens)
            value = gathered[here, :lanes].astype(F32)
            every[here, :] = jnp.where(group == local, value, F32(0)).astype(BF16)

        visit(meta_ref, req_ref, slot_ref, flip, held, requests, tokens, mask)
    source = lax.broadcasted_iota(jnp.int32, (lanes, 2 * rank), 0) % rank
    target = lax.broadcasted_iota(jnp.int32, (lanes, 2 * rank), 1)
    shift = rank if before_ref is not None else 0
    fold = jnp.where(source + shift == target, F32(1), F32(0)).astype(BF16)
    result = jnp.dot(every[...], fold, preferred_element_type=F32)
    if before_ref is not None:
        result = result + before_ref[...].astype(F32)
    out_ref[...] = result.astype(BF16)


def low_rank(meta, req, slot, xs, flips, down_t, before, held, rank, tokens, capacity, deps):
    requests = 2 * capacity
    size = capacity * tokens * len(flips)
    depth = xs[0].shape[1]
    smem = pl.BlockSpec(memory_space=pltpu.SMEM)
    vmem = pl.BlockSpec(memory_space=pltpu.VMEM)
    extra = [] if before is None else [before]
    return pl.pallas_call(
        functools.partial(low_kernel, flips, before is not None, held, rank, requests, tokens),
        in_specs=[smem] * 3 + [vmem] * (len(flips) + 1 + len(extra)) + [pl.BlockSpec(memory_space=pl.ANY)] * len(deps),
        out_specs=vmem,
        out_shape=jax.ShapeDtypeStruct((size, 2 * rank), BF16),
        scratch_shapes=[pltpu.VMEM((size, depth), BF16), pltpu.VMEM((size, held * rank), BF16)],
        compiler_params=pltpu.CompilerParams(vmem_limit_bytes=VMEM_LIMIT),
        cost_estimate=LIGHT,
    )(meta, req, slot, *xs, down_t, *extra, *deps)


def up_kernel(ndeps, held, rank, requests, tokens, meta_ref, req_ref, slot_ref, *refs):
    low_refs, up_ref, out_refs = refs[:4], refs[4], refs[5 + ndeps : 9 + ndeps]
    wide, spread = refs[-2:]
    lanes = held * rank
    half = low_refs[0].shape[0]
    size = half // 2

    @pl.when(pl.program_id(0) == 0)
    def _():
        total = low_refs[0][...].astype(F32)
        for r in low_refs[1:]:
            total = total + r[...].astype(F32)
        total = total.astype(BF16)
        source = lax.broadcasted_iota(jnp.int32, (2 * rank, lanes), 0)
        target = lax.broadcasted_iota(jnp.int32, (2 * rank, lanes), 1) % rank
        for h in range(2):
            tile = jnp.where(source == target + h * rank, F32(1), F32(0)).astype(BF16)
            wide[h * half : (h + 1) * half, :] = jnp.dot(
                total, tile, preferred_element_type=F32
            ).astype(BF16)
        spread[...] = jnp.zeros(spread.shape, BF16)
        group = lax.broadcasted_iota(jnp.int32, (1, lanes), 1) // rank
        for i in range(4):

            def mask(q, row, local, i=i):
                here = pl.ds(i * size + row, tokens)
                value = wide[here, :].astype(F32)
                spread[here, :] = jnp.where(group == local, value, F32(0)).astype(BF16)

            visit(meta_ref, req_ref, slot_ref, i, held, requests, tokens, mask)

    result = jnp.dot(spread[...], up_ref[...], preferred_element_type=F32).astype(BF16)
    for i in range(4):
        out_refs[i][...] = result[i * size : (i + 1) * size, :]


def up_project(meta, req, slot, lows, up_2d, held, rank, tokens, capacity, requests, deps, tile=1024):
    cols = up_2d.shape[1]
    size = capacity * tokens
    smem = pl.BlockSpec(memory_space=pltpu.SMEM)
    return pl.pallas_call(
        functools.partial(up_kernel, len(deps), held, rank, requests, tokens),
        grid=(cols // tile,),
        in_specs=[smem] * 3
        + [pl.BlockSpec(lows[0].shape, lambda j: (0, 0))] * 4
        + [pl.BlockSpec((held * rank, tile), lambda j: (0, j))]
        + [pl.BlockSpec(memory_space=pl.ANY)] * len(deps),
        out_specs=[pl.BlockSpec((size, tile), lambda j: (0, j))] * 4,
        out_shape=[jax.ShapeDtypeStruct((size, cols), BF16)] * 4,
        scratch_shapes=[pltpu.VMEM((4 * size, held * rank), BF16)] * 2,
        compiler_params=pltpu.CompilerParams(vmem_limit_bytes=VMEM_LIMIT),
        cost_estimate=LIGHT,
    )(meta, req, slot, *lows, up_2d, *deps)


def extend_kernel(len_ref, x_ref, out_ref):
    rows, depth = x_ref.shape
    extra = out_ref.shape[0] - rows
    out_ref[:rows, :] = x_ref[...]
    lane = lax.broadcasted_iota(jnp.int32, (extra, depth), 1)
    below = jnp.zeros((extra, depth), F32)
    for q in range(len_ref.shape[0]):
        below = jnp.where(lane == q, len_ref[q].astype(F32), below)
    out_ref[rows:, :] = below.astype(BF16)


def extend(lengths, x, extra):
    vmem = pl.BlockSpec(memory_space=pltpu.VMEM)
    return pl.pallas_call(
        extend_kernel,
        in_specs=[pl.BlockSpec(memory_space=pltpu.SMEM), vmem],
        out_specs=vmem,
        out_shape=jax.ShapeDtypeStruct((x.shape[0] + extra, x.shape[1]), BF16),
        compiler_params=pltpu.CompilerParams(vmem_limit_bytes=SMALL_VMEM),
        cost_estimate=LIGHT,
    )(lengths, x)


def keep_kernel(meta_ref, came_ref, own_ref, *refs):
    out_ref, held, sem = refs[-3:]

    @pl.when(meta_ref[0] == meta_ref[1])
    def _():
        for source, target in ((own_ref, held), (held, out_ref)):
            copy = pltpu.make_async_copy(source, target, sem)
            copy.start()
            copy.wait()


def keep(meta, came, own, deps=()):
    anywhere = pl.BlockSpec(memory_space=pl.ANY)
    return pl.pallas_call(
        keep_kernel,
        in_specs=[pl.BlockSpec(memory_space=pltpu.SMEM)] + [anywhere] * (2 + len(deps)),
        out_specs=anywhere,
        out_shape=jax.ShapeDtypeStruct(came.shape, came.dtype),
        scratch_shapes=[pltpu.VMEM(came.shape, came.dtype), pltpu.SemaphoreType.DMA],
        input_output_aliases={1: 0},
        compiler_params=pltpu.CompilerParams(vmem_limit_bytes=SMALL_VMEM),
        cost_estimate=LIGHT,
    )(meta, came, own, *deps)


def merge_kernel(count, streams, has_back, tail, u_ref, *refs):
    out_ref, tail_ref = (refs[-2], refs[-1]) if tail else (refs[-1], None)
    span = refs[0].shape[0]
    for i in range(count):
        at = 0
        for j in range(streams):
            piece = refs[i * streams + j]
            value = piece[...]
            width = piece.shape[1]
            if has_back:
                back = refs[count * streams + i][:, at : at + width]
                value = (value.astype(F32) + back.astype(F32)).astype(BF16)
            out_ref[i * span : (i + 1) * span, at : at + width] = value
            if tail and i == count - 1:
                tail_ref[:, at : at + width] = value
            at += width


def merge(u, pieces, backs, steps_of, tail=False, deps=()):
    count, streams = len(steps_of), len(pieces) // len(steps_of)
    span = pieces[0].shape[0]
    cols = sum(p.shape[1] for p in pieces[:streams])

    def spec_of(low, high, k):
        return pl.BlockSpec((span, cols), lambda i, r: (jnp.clip(k - r[0], low, high) - low, 0))

    specs = [pl.BlockSpec(p.shape, lambda i, r: (0, 0)) for p in pieces]
    specs += [spec_of(low, high, k) for k, (_, low, high) in zip(steps_of, backs)]
    specs += [pl.BlockSpec(memory_space=pl.ANY)] * len(deps)
    sizes = [count * span] + [span] * tail
    return pl.pallas_call(
        functools.partial(merge_kernel, count, streams, bool(backs), tail),
        grid_spec=pltpu.PrefetchScalarGridSpec(
            num_scalar_prefetch=1,
            grid=(1,),
            in_specs=specs,
            out_specs=[pl.BlockSpec((n, cols), lambda i, r: (0, 0)) for n in sizes],
        ),
        out_shape=[jax.ShapeDtypeStruct((n, cols), BF16) for n in sizes],
        compiler_params=pltpu.CompilerParams(vmem_limit_bytes=SMALL_VMEM),
        cost_estimate=LIGHT,
    )(u, *pieces, *[b[0] for b in backs], *deps)


def finish_kernel(n, sizes, first, span, held, requests, tokens, capacity, with_delta, with_acc, *refs):
    meta_ref, req_ref, slot_ref = refs[:3]
    len_refs = refs[3:7]
    at = 7
    value_refs, got_refs = refs[at : at + n], refs[at + n : at + 2 * n]
    at += 2 * n
    delta_refs = refs[at : at + 4] if with_delta else ()
    at += len(delta_refs)
    acc_ref = refs[at] if with_acc else None
    out_ref, picks, dpicks = refs[-3:]
    s, t, _, _ = where_am_i(meta_ref)
    size = capacity * tokens
    keep = (s == t) | (s == (t ^ 2))

    @pl.when(pl.program_id(0) == 0)
    def _():
        flip = 2 * (t // 2)
        key = s ^ flip
        start = jnp.where((t == 0) | (t == 3), 3, 2) * span - first
        for i in range(1, 4):
            start = start + jnp.where(((s ^ i) ^ flip) < key, total_of(len_refs[i]), 0)
        depth = picks.shape[1]
        token = lax.broadcasted_iota(jnp.int32, (tokens, depth), 0)
        base = lax.broadcasted_iota(jnp.int32, (tokens, depth), 1) - token
        wide = dpicks.shape[1]
        dtoken = lax.broadcasted_iota(jnp.int32, (tokens, wide), 0)
        dbase = lax.broadcasted_iota(jnp.int32, (tokens, wide), 1) - dtoken
        counts = [jnp.int32(0)] * 4
        for q in range(requests):
            length = len_refs[0][q]
            here = (base == start) & (token < length)
            picks[q * tokens : (q + 1) * tokens, :] = jnp.where(here, F32(1), F32(0)).astype(BF16)
            start = start + length
            if with_delta:
                owner = lax.div(slot_ref[req_ref[s * requests + q]], held) ^ s
                turn = jnp.int32(0)
                for i in range(4):
                    turn = turn + jnp.where(owner == i, counts[i], 0)
                    counts[i] = counts[i] + jnp.where(owner == i, 1, 0)
                here = (dbase == owner * size + turn * tokens) & (dtoken < length)
                dpicks[q * tokens : (q + 1) * tokens, :] = jnp.where(here, F32(2), F32(0)).astype(BF16)

    def run(group):
        total = None
        for i, (ref, count) in enumerate(zip(group, sizes)):
            offset = sum(sizes[:i])
            part = jnp.dot(picks[:, offset : offset + count], ref[...], preferred_element_type=F32)
            total = part if total is None else total + part
        if with_delta:
            stack = jnp.concatenate([r[...] for r in delta_refs], axis=0)
            total = total + jnp.dot(dpicks[...], stack, preferred_element_type=F32)
        if with_acc:
            total = total + acc_ref[...]
        out_ref[...] = total.astype(out_ref.dtype)

    @pl.when(keep)
    def _():
        run(value_refs)

    @pl.when(jnp.logical_not(keep))
    def _():
        run(got_refs)


def finish(meta, req, slot, lens, values, gots, first, deltas, acc, out_dtype, span, held, tokens, capacity, deps=(), tile=1024):
    requests = lens[0].shape[0]
    rows = requests * tokens
    cols = values[0].shape[1]
    sizes = [v.shape[0] for v in values]
    depth = sum(sizes)
    wide = 4 * capacity * tokens
    smem = pl.BlockSpec(memory_space=pltpu.SMEM)
    big = list(values) + list(gots) + list(deltas) + ([] if acc is None else [acc])
    return pl.pallas_call(
        functools.partial(
            finish_kernel,
            len(sizes), sizes, first, span, held, requests, tokens, capacity, bool(deltas), acc is not None,
        ),
        grid=(cols // tile,),
        in_specs=[smem] * 7
        + [pl.BlockSpec((a.shape[0], tile), lambda j: (0, j)) for a in big]
        + [pl.BlockSpec(memory_space=pl.ANY)] * len(deps),
        out_specs=pl.BlockSpec((rows, tile), lambda j: (0, j)),
        out_shape=jax.ShapeDtypeStruct((rows, cols), out_dtype),
        scratch_shapes=[
            pltpu.VMEM((rows, depth), BF16),
            pltpu.VMEM((rows, wide if deltas else 128), BF16),
        ],
        compiler_params=pltpu.CompilerParams(vmem_limit_bytes=SMALL_VMEM),
        cost_estimate=LIGHT,
    )(meta, req, slot, *lens, *big, *deps)


def on_store(value, flip):
    return lax.ppermute(value, "store", [(i, i ^ flip) for i in range(4)])


def plane(s, u):
    return u if s >= 2 else 3 - u


def last_step(s):
    return 3 if s in (0, 3) else 2


def on_mesh(value, pairs):
    return lax.ppermute(value, ("tensor", "store"), [(a * 4 + b, c * 4 + d) for (a, b), (c, d) in pairs])


def square(x, w, down, up, req, slot, lengths):
    requests, tokens, depth = x.shape
    cols = w.shape[1]
    rows = requests * tokens
    live = 3 * rows
    held, _, rank = down.shape
    capacity = requests // 2
    span = SPAN
    steps = live // span
    edge = cols // 2 + 128
    bounds = ((0, edge), (edge, cols))

    s = lax.axis_index("store")
    t = lax.axis_index("tensor")
    meta = jnp.stack([s, t]).astype(jnp.int32)

    x_me = x.reshape(rows, depth)
    x_out = extend(lengths, x_me, tokens)
    x_far = on_store(x_out, 2)
    x_sib = on_store(x_out, 1)

    def lengths_of(array):
        return array[rows, :requests].astype(jnp.int32)

    lens = [lengths, lengths_of(x_sib)]
    xs = [x_me, x_sib]
    down_t = jnp.transpose(down, (0, 2, 1)).reshape(held * rank, depth)
    up_2d = up.reshape(held * rank, cols)

    early = rows // span
    back_pairs = [((plane(b, 3), b), (plane(b, 2), b)) for b in (1, 2)]
    across = [((v, v), (v, v ^ 2)) for v in range(4)]
    beside = [((v, v), (v, v ^ 1)) for v in range(4)] + [((v, v ^ 2), (v, v ^ 3)) for v in range(4)]
    chip = s // 2
    u = jnp.where(chip == 1, t, 3 - t)

    final, carry, parts = {}, [None] * STREAMS, {}

    def chunk_of(source, k, j):
        c = jnp.clip(k - u, 0, steps - 1)
        at = jnp.where(c < early, c + steps - early, c - early) * span
        lo, hi = bounds[j]
        return lax.dynamic_slice(source, (at, lo), (span, hi - lo))

    def first_chunk(c, j):
        at = (c + steps - early) * span
        return parts[0][at : at + span, bounds[j][0] : bounds[j][1]]

    def pairs_of(k):
        return [
            ((plane(b, v), b), (plane(b, v + 1), b))
            for b in range(4)
            for v in range(last_step(b))
            if 0 <= k - v < steps
        ]

    last_pairs = pairs_of(steps + 1)

    def chain_step(k, *deps, both=False):
        pairs = pairs_of(k)
        for j in range(STREAMS):
            if k < early:
                value = first_chunk(0, j)
                for c in range(1, k + 1):
                    value = jnp.where(k - u >= c, first_chunk(c, j), value)
            else:
                value = chunk_of(parts[1], k, j)
            if carry[j] is not None:
                came = carry[j]
                if deps and (both or not j):
                    came = after(came, *deps)
                total = value.astype(F32) + came.astype(F32)
                value = total.astype(BF16)
            final[k, j] = value
            carry[j] = on_mesh(value, pairs) if k < steps + 1 else None

    values, gots = [], []

    def merged(lo, hi, tail=False, deps=()):
        ks = range(lo, hi)
        backs = []
        if hi <= steps + 2:
            for k in ks:
                backs.append(next(b for b in back if b[1] <= k - 2 <= b[2]))
        return merge(u_vec, [final[k, j] for k in ks for j in range(STREAMS)], backs, ks, tail, deps)

    def cross(value):
        return on_mesh(value, across), value

    def hand_on(value):
        values.append(value)
        gots.append(on_mesh(value, beside))

    u_vec = u.astype(jnp.int32).reshape(1)
    parts[0] = project(meta, lens[:2], xs[:2], w, 0, rows, live, live // rows - 1)
    chain_step(0)
    low = low_rank(
        meta, req, slot, xs[:2], (0, 1), down_t, None, held, rank, tokens, capacity, (parts[0],)
    )
    chain_step(1)
    x_far = after(x_far, final[1, 0], final[1, 1], low)
    x_fsib = on_store(x_far, 1)
    xs = [x_me, x_sib, x_far, x_fsib]
    lens = lens + [lengths_of(x_far), lengths_of(x_fsib)]
    parts[1] = project(
        meta, lens, xs, w, rows, live - rows, live, 0, parts[0], (final[1, 0], final[1, 1])
    )
    chain_step(2)
    low = low_rank(
        meta, req, slot, xs[2:], (2, 3), down_t, low, held, rank, tokens, capacity, (final[2, 0], final[2, 1])
    )
    lows = [low] + [lax.ppermute(low, "tensor", [(i, i ^ f) for i in range(4)]) for f in (3, 1, 2)]
    chain_step(3, low, both=True)
    delta = up_project(
        meta, req, slot, lows, up_2d, held, rank, tokens, capacity, requests, (final[3, 0], final[3, 1])
    )
    deltas = [delta[0]] + [on_store(delta[i], i) for i in (1, 2, 3)]
    chain_step(4, delta[0])

    def send_back(low, high, *deps):
        at = (low - early if low >= early else low + steps - early) * span
        rows_of = after(parts[1][at : at + (high + 1 - low) * span], *deps)
        return on_mesh(rows_of, back_pairs), low, high

    back = [send_back(early, steps - 1, final[4, 0], final[4, 1])]
    chain_step(5, deltas[1])
    back.append(send_back(0, early - 1, final[5, 0], final[5, 1]))
    chain_step(6, deltas[2])
    (two,) = merged(4, 6)
    (one,) = merged(2, 4, deps=(two,))
    hand_on(one)
    chain_step(7, two, deltas[3], both=True)
    two = keep(meta, *cross(two))
    three, last = merged(6, 8, True)
    came = on_mesh(last, last_pairs)
    three = cross(three)
    (four,) = merge(u_vec, [came], [(parts[1], early, steps - 1)], [steps + 2], deps=(two,))
    hand_on(two)
    partial = finish(
        meta, req, slot, lens, values[:1], gots[:1], 2 * span, deltas, None, F32, span, held, tokens, capacity,
        (four,),
    )
    hand_on(keep(meta, *three, (partial,)))
    hand_on(keep(meta, *cross(four)))
    out = finish(
        meta, req, slot, lens, values[1:], gots[1:], 4 * span, (), partial, BF16, span, held, tokens, capacity
    )
    return out.reshape(requests, tokens, cols)


def solution(mesh):
    in_specs = (
        P(("groups", "store"), None, "tensor"),
        P("tensor", "store"),
        P("store", "tensor", None),
        P("store", None, "tensor"),
        P("groups"),
        P("groups"),
        P(("groups", "store")),
    )
    out_specs = P(("groups", "store"), None, "tensor")
    four = mesh.shape["store"] == 4 and mesh.shape["tensor"] == 4
    body = square if four else general
    return jax.shard_map(body, mesh=mesh, in_specs=in_specs, out_specs=out_specs, check_vma=False)
```
